1024 devices in a mesh: dp: 128 (over x_hi, z, core), emb: 8 (over y, x_lo).
Axes of the slice: x: 4 (x_hi: 2, x_lo: 2; x = x_hi * 2 + x_lo), y: 4, z: 32, core: 2. Of those that a mesh axis runs over, the one named last changes fastest.
Arguments:
- img_feat: bfloat16 [65536, 1152], P('dp'), may hold values from -6 to 6
- w_proj: bfloat16 [1152, 1152], P(None, 'emb'), may hold values from -0.1875 to 0.1875
- txt_emb: bfloat16 [65536, 1152], P(('dp', 'emb')), may hold values from -0.19921875 to 0.19921875
- logit_scale: float32 [1], replicated, may hold values from 1 to 3
- logit_bias: float32 [1], replicated, may hold values from -3 to -1
Outputs:
- d_weight: float32 [1152, 1152], P(None, 'emb')
- d_text: float32 [65536, 1152], P(('dp', 'emb'))
The draws below stay inside these ranges and needn't reach their ends.
All inputs are finite; a program needn't handle non-finite values.
Results may differ from the reference program's by a relative error of at most 0.0059.
Values may be sent and summed in bfloat16 or wider, within the bound.
No kernel may reach another device: no remote copies, remote signals or barrier semaphores. Data moves between devices by JAX's collectives and lax.ppermute only.
A program may use at most 32 MiB of HBM per device.

```python
import jax
import jax.numpy as jnp
from jax import lax

D = 1152
STEPS = 3
BATCH = 65536
N_DP = 128


def block_levels(key, extent, split, low, top_value):
    factor_of, own = 1.0, jax.random.fold_in(key, 6)
    for position, shards_of in split:
        steps = jnp.exp(jax.random.uniform(jax.random.fold_in(own, position), (shards_of,), jnp.float32, low / len(split), top_value / len(split)))
        factor_of = factor_of * jnp.repeat(steps, extent[position] // shards_of).reshape([-1 if axis == position else 1 for axis in range(len(extent))])
    return factor_of


def noise(own_key, shape, scale, bound, cuts=(), held_as=jnp.bfloat16):
    drawn = scale * jax.random.normal(own_key, shape, jnp.float32)
    if cuts:
        drawn = drawn * block_levels(own_key, shape, cuts, -0.22, 0.18)
    return jnp.clip(drawn, -bound, bound).astype(held_as)


def setup_inputs(seed: int = 0) -> dict:
    key_of = jax.random.split(jax.random.key(seed), 6)
    img_feat = noise(key_of[0], (BATCH, D), 1.0, 6.0, ((0, 128),))
    w_proj = noise(key_of[1], (D, D), D ** -0.5, 0.1875, ((1, 8),))
    txt_emb = noise(key_of[2], (BATCH, D), 0.03, 0.19921875, ((0, 1024),))
    logit_scale = jnp.clip(jax.random.uniform(key_of[3], (1,), jnp.float32, 1.0, 3.0), 1.0, 3.0)
    logit_bias = jnp.clip(jax.random.uniform(key_of[4], (1,), jnp.float32, -3.0, -1.0), -3.0, -1.0)
    return {"img_feat": img_feat, "w_proj": w_proj, "txt_emb": txt_emb, "logit_scale": logit_scale, "logit_bias": logit_bias}


epsilon = 1e-06

def unit_rows(values):
    widened = values.astype(jnp.float32)
    inverse = lax.rsqrt(lax.optimization_barrier(jnp.sum(widened * widened, axis=1, keepdims=True)) + epsilon)
    return (widened * inverse, inverse)

def reference(img_feat, w_proj, txt_emb, logit_scale, logit_bias):
    projected = jnp.dot(img_feat, w_proj, preferred_element_type=jnp.float32).astype(jnp.bfloat16)
    unit_img, inv_img = unit_rows(projected)
    z_img = unit_img.astype(jnp.bfloat16)
    unit_txt, inv_txt = unit_rows(txt_emb)
    z_txt = unit_txt.astype(jnp.bfloat16)
    shard_rows = z_img.shape[0] // N_DP
    width = z_img.shape[1]
    img_shards = z_img.reshape(N_DP, shard_rows, width)
    txt_shards = z_txt.reshape(N_DP, shard_rows, width)
    multiplier = logit_scale[0]
    offset = logit_bias[0]
    diagonal = jnp.eye(shard_rows, dtype=bool)
    grad_img = jnp.zeros((N_DP, shard_rows, width), jnp.float32)
    grad_txt = jnp.zeros((N_DP, shard_rows, width), jnp.float32)
    for distance in range(STEPS):
        shifted = jnp.roll(txt_shards, distance, axis=0)
        if distance == 0:
            signs = jnp.where(diagonal, 1.0, -1.0).astype(jnp.float32)
        else:
            signs = jnp.full((shard_rows, shard_rows), -1.0, jnp.float32)

        def pair_block(pair):
            img_block, txt_block = pair
            cosines = lax.dot_general(img_block, txt_block, (((1,), (1,)), ((), ())), preferred_element_type=jnp.float32)
            logits = multiplier * cosines + offset
            pair_grad = (-signs * jax.nn.sigmoid(-signs * logits)).astype(jnp.bfloat16)
            img_term = multiplier * jnp.dot(pair_grad, txt_block, preferred_element_type=jnp.float32)
            txt_term = multiplier * lax.dot_general(pair_grad, img_block, (((0,), (0,)), ((), ())), preferred_element_type=jnp.float32)
            return (img_term, txt_term)
        img_term, txt_term = lax.map(pair_block, (img_shards, shifted))
        grad_img = grad_img + img_term
        grad_txt = grad_txt + jnp.roll(txt_term, -distance, axis=0)
    grad_img = grad_img.reshape(N_DP * shard_rows, width)
    grad_txt = grad_txt.reshape(N_DP * shard_rows, width)
    inner_img = lax.optimization_barrier(jnp.sum(unit_img * grad_img, axis=1, keepdims=True))
    grad_proj = (inv_img * (grad_img - unit_img * inner_img)).astype(jnp.bfloat16)
    d_weight = lax.dot_general(img_feat, grad_proj, (((0,), (0,)), ((), ())), preferred_element_type=jnp.float32)
    inner_txt = lax.optimization_barrier(jnp.sum(unit_txt * grad_txt, axis=1, keepdims=True))
    d_text = inv_txt * (grad_txt - unit_txt * inner_txt)
    return (d_weight, d_text)
```

```python
import jax
import jax.numpy as jnp
from jax import lax
from jax.sharding import PartitionSpec as P

STEPS = 3
EPSILON = 1e-06
LANES = 128
UNIT = 16


def passed_along(array, axis, by):
    count = lax.axis_size(axis)
    return lax.ppermute(array, axis, [(i, (i + by) % count) for i in range(count)])


def line_groups(count):
    z_len = count // 4
    index = lambda hi, z, core: (hi * z_len + z) * 2 + core
    lines = [[index(hi, z, c) for z in range(z_len)] for hi in range(2) for c in range(2)]
    quads = [[index(hi, z, c) for hi in range(2) for c in range(2)] for z in range(z_len)]
    return z_len, lines, quads


def swap(parts, axis, groups=None):
    return lax.all_to_all(parts, axis, 0, 0, axis_index_groups=groups)


def gathered(part, count, axis, groups=None):
    return swap(jnp.broadcast_to(part[None], (count,) + part.shape), axis, groups)


def summed(parts):
    return jnp.sum(parts.astype(jnp.float32), axis=0)


def sum_over_dp(grad_t):
    width, features = grad_t.shape
    tiles = features // LANES
    z_len, lines, quads = line_groups(lax.axis_size("dp"))
    units = tiles * width // UNIT
    per_quad = -(-units // 4)
    rows = jnp.concatenate(
        [grad_t[:, LANES * t : LANES * (t + 1)] for t in range(tiles)], axis=0
    ).astype(jnp.bfloat16)
    rows = jnp.pad(rows, ((0, (4 * per_quad - units) * UNIT), (0, 0)))
    quad = summed(swap(rows.reshape(4, per_quad * UNIT, LANES), "dp", quads)).astype(jnp.bfloat16)
    per_line = -(-per_quad // z_len)
    quad = jnp.pad(quad, ((0, (z_len * per_line - per_quad) * UNIT), (0, 0)))
    line = summed(swap(quad.reshape(z_len, per_line * UNIT, LANES), "dp", lines))
    back = gathered(line.astype(jnp.bfloat16), z_len, "dp", lines)
    back = back.reshape(z_len * per_line * UNIT, LANES)[: per_quad * UNIT]
    whole = gathered(back, 4, "dp", quads).reshape(4 * per_quad * UNIT, LANES)[: units * UNIT]
    whole = whole.astype(jnp.float32).reshape(tiles, width, LANES)
    return jnp.swapaxes(whole, 1, 2).reshape(features, width)


def local(img_feat, w_proj, txt_emb, logit_scale, logit_bias):
    image_rows, features = img_feat.shape
    text_rows = txt_emb.shape[0]
    width = w_proj.shape[1]
    members = lax.axis_size("emb")
    member = lax.axis_index("emb")
    scale = logit_scale[0]
    offset = logit_bias[0]

    wide_txt = txt_emb.astype(jnp.float32)
    inv_txt = lax.rsqrt(jnp.sum(wide_txt * wide_txt, axis=1, keepdims=True) + EPSILON)
    unit_txt = wide_txt * inv_txt
    z_txt = unit_txt.astype(jnp.bfloat16)
    visitors = [z_txt] + [passed_along(z_txt, "dp", k) for k in range(1, STEPS)]

    local_proj = lax.dot_general(
        w_proj, img_feat, (((0,), (1,)), ((), ())), preferred_element_type=jnp.float32
    ).astype(jnp.bfloat16)
    projected = gathered(local_proj, members, "emb").reshape(features, image_rows)
    wide_img = projected.astype(jnp.float32)
    inv_img = lax.rsqrt(jnp.sum(wide_img * wide_img, axis=0, keepdims=True) + EPSILON)
    unit_img = wide_img * inv_img
    z_img = unit_img.astype(jnp.bfloat16)

    texts = jnp.concatenate(visitors, axis=0)
    cosines = jnp.dot(texts, z_img, preferred_element_type=jnp.float32)
    text_index = lax.broadcasted_iota(jnp.int32, cosines.shape, 0)
    image_index = lax.broadcasted_iota(jnp.int32, cosines.shape, 1)
    own = (text_index < text_rows) & (image_index == member * text_rows + text_index)
    signs = jnp.where(own, 1.0, -1.0)
    pair_grad = (-signs * jax.nn.sigmoid(-signs * (scale * cosines + offset))).astype(jnp.bfloat16)
    inner_img = jnp.sum(pair_grad.astype(jnp.float32) * cosines, axis=0, keepdims=True)

    txt_terms = scale * lax.dot_general(
        pair_grad, z_img, (((1,), (1,)), ((), ())), preferred_element_type=jnp.float32
    )
    sent = [
        passed_along(txt_terms[k * text_rows : (k + 1) * text_rows].astype(jnp.bfloat16), "dp", -k)
        for k in range(1, STEPS)
    ]

    grad_img = lax.dot_general(
        texts, pair_grad, (((0,), (0,)), ((), ())), preferred_element_type=jnp.float32
    )
    grad_proj = (scale * inv_img) * (grad_img - unit_img * inner_img)
    parts = grad_proj.astype(jnp.bfloat16).reshape(members, width, image_rows)
    grad_part = summed(swap(parts, "emb")).astype(jnp.bfloat16)
    local_weight = jnp.dot(grad_part, img_feat, preferred_element_type=jnp.float32)
    d_weight = sum_over_dp(local_weight)

    grad_txt = txt_terms[:text_rows]
    for term in sent:
        grad_txt = grad_txt + term.astype(jnp.float32)
    inner_txt = jnp.sum(unit_txt * grad_txt, axis=1, keepdims=True)
    d_text = inv_txt * (grad_txt - unit_txt * inner_txt)
    return (d_weight, d_text)


def solution(mesh):
    in_specs = (P("dp", None), P(None, "emb"), P(("dp", "emb"), None), P(), P())
    out_specs = (P(None, "emb"), P(("dp", "emb"), None))
    return jax.shard_map(local, mesh=mesh, in_specs=in_specs, out_specs=out_specs, check_vma=False)
```

```python
import jax
import jax.numpy as jnp
from jax import lax
from jax.sharding import PartitionSpec as P

STEPS = 3
EPSILON = 1e-06
LANES = 128
ROWS = 8


def passed_along(array, axis, by):
    count = lax.axis_size(axis)
    return lax.ppermute(array, axis, [(i, (i + by) % count) for i in range(count)])


def dp_groups(count):
    z_len = count // 4
    index = lambda hi, z, core: (hi * z_len + z) * 2 + core
    near = [
        [index(hi, z + dz, c) for hi in range(2) for dz in range(2) for c in range(2)]
        for z in range(0, z_len, 2)
    ]
    far = [list(members) for members in zip(*near)]
    return near, far


def swap(parts, axis, groups=None):
    return lax.all_to_all(parts, axis, 0, 0, axis_index_groups=groups)


def gathered(part, count, axis, groups=None):
    return swap(jnp.broadcast_to(part[None], (count,) + part.shape), axis, groups)


def summed(parts):
    return jnp.sum(parts.astype(jnp.float32), axis=0)


def sum_over_dp(grad_t):
    width, features = grad_t.shape
    tiles = features // LANES
    near, far = dp_groups(lax.axis_size("dp"))
    count = len(near[0])
    share = -(-tiles * width // (count * ROWS)) * ROWS
    rows = jnp.concatenate(
        [grad_t[:, LANES * t : LANES * (t + 1)] for t in range(tiles)], axis=0
    ).astype(jnp.bfloat16)
    rows = jnp.pad(rows, ((0, count * share - tiles * width), (0, 0)))
    part = summed(swap(rows.reshape(count, share, LANES), "dp", near)).astype(jnp.bfloat16)
    total = summed(lax.all_gather(part, "dp", axis=0, axis_index_groups=far)).astype(jnp.bfloat16)
    whole = gathered(total, count, "dp", near).reshape(count * share, LANES)[: tiles * width]
    whole = whole.astype(jnp.float32).reshape(tiles, width, LANES)
    return jnp.swapaxes(whole, 1, 2).reshape(features, width)


def local(img_feat, w_proj, txt_emb, logit_scale, logit_bias):
    image_rows, features = img_feat.shape
    text_rows = txt_emb.shape[0]
    width = w_proj.shape[1]
    members = lax.axis_size("emb")
    member = lax.axis_index("emb")
    scale = logit_scale[0]
    offset = logit_bias[0]

    wide_txt = txt_emb.astype(jnp.float32)
    inv_txt = lax.rsqrt(jnp.sum(wide_txt * wide_txt, axis=1, keepdims=True) + EPSILON)
    unit_txt = wide_txt * inv_txt
    z_txt = unit_txt.astype(jnp.bfloat16)
    visitors = [z_txt] + [passed_along(z_txt, "dp", k) for k in range(1, STEPS)]

    local_proj = lax.dot_general(
        w_proj, img_feat, (((0,), (1,)), ((), ())), preferred_element_type=jnp.float32
    ).astype(jnp.bfloat16)
    projected = gathered(local_proj, members, "emb").reshape(features, image_rows)
    wide_img = projected.astype(jnp.float32)
    inv_img = lax.rsqrt(jnp.sum(wide_img * wide_img, axis=0, keepdims=True) + EPSILON)
    unit_img = wide_img * inv_img
    z_img = unit_img.astype(jnp.bfloat16)

    texts = jnp.concatenate(visitors, axis=0)
    cosines = jnp.dot(texts, z_img, preferred_element_type=jnp.float32)
    text_index = lax.broadcasted_iota(jnp.int32, cosines.shape, 0)
    image_index = lax.broadcasted_iota(jnp.int32, cosines.shape, 1)
    own = (text_index < text_rows) & (image_index == member * text_rows + text_index)
    signs = jnp.where(own, 1.0, -1.0)
    pair_grad = (-signs * jax.nn.sigmoid(-signs * (scale * cosines + offset))).astype(jnp.bfloat16)
    inner_img = jnp.sum(pair_grad.astype(jnp.float32) * cosines, axis=0, keepdims=True)

    txt_terms = scale * lax.dot_general(
        pair_grad, z_img, (((1,), (1,)), ((), ())), preferred_element_type=jnp.float32
    )
    sent = [
        passed_along(txt_terms[k * text_rows : (k + 1) * text_rows].astype(jnp.bfloat16), "dp", -k)
        for k in range(1, STEPS)
    ]

    grad_img = lax.dot_general(
        texts, pair_grad, (((0,), (0,)), ((), ())), preferred_element_type=jnp.float32
    )
    grad_proj = (scale * inv_img) * (grad_img - unit_img * inner_img)
    parts = grad_proj.astype(jnp.bfloat16).reshape(members, width, image_rows)
    grad_part = summed(swap(parts, "emb")).astype(jnp.bfloat16)
    local_weight = jnp.dot(grad_part, img_feat, preferred_element_type=jnp.float32)
    d_weight = sum_over_dp(local_weight)

    grad_txt = txt_terms[:text_rows]
    for term in sent:
        grad_txt = grad_txt + term.astype(jnp.float32)
    inner_txt = jnp.sum(unit_txt * grad_txt, axis=1, keepdims=True)
    d_text = inv_txt * (grad_txt - unit_txt * inner_txt)
    return (d_weight, d_text)


def solution(mesh):
    in_specs = (P("dp", None), P(None, "emb"), P(("dp", "emb"), None), P(), P())
    out_specs = (P(None, "emb"), P(("dp", "emb"), None))
    return jax.shard_map(local, mesh=mesh, in_specs=in_specs, out_specs=out_specs, check_vma=False)
```

```python
import jax
import jax.numpy as jnp
from jax import lax
from jax.sharding import PartitionSpec as P

STEPS = 3
EPSILON = 1e-06
LANES = 128
ROWS = 8


def passed_along(array, axis, by):
    count = lax.axis_size(axis)
    return lax.ppermute(array, axis, [(i, (i + by) % count) for i in range(count)])


def dp_groups(count):
    z_len = count // 4
    index = lambda hi, z, core: (hi * z_len + z) * 2 + core
    near = [
        [index(hi, z + dz, c) for hi in range(2) for dz in range(2) for c in range(2)]
        for z in range(0, z_len, 2)
    ]
    far = [list(members) for members in zip(*near)]
    return near, far


def swap(parts, axis, groups=None):
    return lax.all_to_all(parts, axis, 0, 0, axis_index_groups=groups)


def gathered(part, count, axis, groups=None):
    return swap(jnp.broadcast_to(part[None], (count,) + part.shape), axis, groups)


def summed(parts):
    return jnp.sum(parts.astype(jnp.float32), axis=0)


def sum_over_dp(grad_t, early):
    width, features = grad_t.shape
    tiles = features // LANES
    near, far = dp_groups(lax.axis_size("dp"))
    count = len(near[0])
    share = -(-tiles * width // (count * ROWS)) * ROWS
    rows = jnp.concatenate(
        [grad_t[:, LANES * t : LANES * (t + 1)] for t in range(tiles)], axis=0
    ).astype(jnp.bfloat16)
    rows = jnp.pad(rows, ((0, count * share - tiles * width), (0, 0)))
    part = summed(swap(rows.reshape(count, share, LANES), "dp", near)).astype(jnp.bfloat16)
    part, early = lax.optimization_barrier((part, early))
    total = summed(lax.all_gather(part, "dp", axis=0, axis_index_groups=far)).astype(jnp.bfloat16)
    whole = gathered(total, count, "dp", near).reshape(count * share, LANES)[: tiles * width]
    whole = whole.astype(jnp.float32).reshape(tiles, width, LANES)
    return jnp.swapaxes(whole, 1, 2).reshape(features, width), early


def local(img_feat, w_proj, txt_emb, logit_scale, logit_bias):
    image_rows, features = img_feat.shape
    text_rows = txt_emb.shape[0]
    width = w_proj.shape[1]
    members = lax.axis_size("emb")
    member = lax.axis_index("emb")
    scale = logit_scale[0]
    offset = logit_bias[0]

    wide_txt = txt_emb.astype(jnp.float32)
    inv_txt = lax.rsqrt(jnp.sum(wide_txt * wide_txt, axis=1, keepdims=True) + EPSILON)
    unit_txt = wide_txt * inv_txt
    z_txt = unit_txt.astype(jnp.bfloat16)
    visitors = [z_txt] + [passed_along(z_txt, "dp", k) for k in range(1, STEPS)]

    local_proj = lax.dot_general(
        w_proj, img_feat, (((0,), (1,)), ((), ())), preferred_element_type=jnp.float32
    ).astype(jnp.bfloat16)
    projected = gathered(local_proj, members, "emb").reshape(features, image_rows)
    wide_img = projected.astype(jnp.float32)
    inv_img = lax.rsqrt(jnp.sum(wide_img * wide_img, axis=0, keepdims=True) + EPSILON)
    unit_img = wide_img * inv_img
    z_img = unit_img.astype(jnp.bfloat16)

    texts = jnp.concatenate(visitors, axis=0)
    cosines = jnp.dot(texts, z_img, preferred_element_type=jnp.float32)
    text_index = lax.broadcasted_iota(jnp.int32, cosines.shape, 0)
    image_index = lax.broadcasted_iota(jnp.int32, cosines.shape, 1)
    own = (text_index < text_rows) & (image_index == member * text_rows + text_index)
    signs = jnp.where(own, 1.0, -1.0)
    pair_grad = (-signs * jax.nn.sigmoid(-signs * (scale * cosines + offset))).astype(jnp.bfloat16)
    inner_img = jnp.sum(pair_grad.astype(jnp.float32) * cosines, axis=0, keepdims=True)

    txt_terms = scale * lax.dot_general(
        pair_grad, z_img, (((1,), (1,)), ((), ())), preferred_element_type=jnp.float32
    )
    sent = [
        passed_along(txt_terms[k * text_rows : (k + 1) * text_rows].astype(jnp.bfloat16), "dp", -k)
        for k in range(1, STEPS)
    ]

    grad_img = lax.dot_general(
        texts, pair_grad, (((0,), (0,)), ((), ())), preferred_element_type=jnp.float32
    )
    grad_proj = (scale * inv_img) * (grad_img - unit_img * inner_img)
    parts = grad_proj.astype(jnp.bfloat16).reshape(members, width, image_rows)
    grad_part = summed(swap(parts, "emb")).astype(jnp.bfloat16)
    local_weight = jnp.dot(grad_part, img_feat, preferred_element_type=jnp.float32)
    d_weight, sent = sum_over_dp(local_weight, sent)

    grad_txt = txt_terms[:text_rows]
    for term in sent:
        grad_txt = grad_txt + term.astype(jnp.float32)
    inner_txt = jnp.sum(unit_txt * grad_txt, axis=1, keepdims=True)
    d_text = inv_txt * (grad_txt - unit_txt * inner_txt)
    return (d_weight, d_text)


def solution(mesh):
    in_specs = (P("dp", None), P(None, "emb"), P(("dp", "emb"), None), P(), P())
    out_specs = (P(None, "emb"), P(("dp", "emb"), None))
    return jax.shard_map(local, mesh=mesh, in_specs=in_specs, out_specs=out_specs, check_vma=False)
```

```python
import jax
import jax.numpy as jnp
from jax import lax
from jax.sharding import PartitionSpec as P

STEPS = 3
EPSILON = 1e-06
LANES = 128
ROWS = 8
PAIR = 2


def passed_along(array, axis, by):
    count = lax.axis_size(axis)
    return lax.ppermute(array, axis, [(i, (i + by) % count) for i in range(count)])


def to_partner(array):
    return lax.ppermute(array, "emb", [(i, i ^ 1) for i in range(lax.axis_size("emb"))])


def dp_groups(count):
    z_len = count // 4
    index = lambda hi, z, core: (hi * z_len + z) * 2 + core
    near = [
        [index(hi, z + dz, c) for hi in range(2) for dz in range(2) for c in range(2)]
        for z in range(0, z_len, 2)
    ]
    far = [list(members) for members in zip(*near)]
    return near, far


def swap(parts, axis, groups=None):
    return lax.all_to_all(parts, axis, 0, 0, axis_index_groups=groups)


def gathered(part, count, axis, groups=None):
    return swap(jnp.broadcast_to(part[None], (count,) + part.shape), axis, groups)


def summed(parts):
    return jnp.sum(parts.astype(jnp.float32), axis=0)


def sum_over_dp(grad_t, early):
    width, features = grad_t.shape
    tiles = features // LANES
    near, far = dp_groups(lax.axis_size("dp"))
    count = len(near[0])
    share = -(-tiles * width // (count * ROWS)) * ROWS
    slabs = [grad_t[:, LANES * t : LANES * (t + 1)].astype(jnp.bfloat16) for t in range(tiles)]
    slabs.append(jnp.zeros((count * share - tiles * width, LANES), jnp.bfloat16))
    rows = jnp.concatenate(slabs, axis=0)
    part = summed(swap(rows.reshape(count, share, LANES), "dp", near)).astype(jnp.bfloat16)
    part, early = lax.optimization_barrier((part, early))
    total = summed(lax.all_gather(part, "dp", axis=0, axis_index_groups=far)).astype(jnp.bfloat16)
    whole = gathered(total, count, "dp", near).reshape(count * share, LANES)[: tiles * width]
    whole = whole.astype(jnp.float32).reshape(tiles, width, LANES)
    return jnp.swapaxes(whole, 1, 2).reshape(features, width), early


def local(img_feat, w_proj, txt_emb, logit_scale, logit_bias):
    image_rows, features = img_feat.shape
    text_rows = txt_emb.shape[0]
    width = w_proj.shape[1]
    members = lax.axis_size("emb")
    member = lax.axis_index("emb")
    half_rows = image_rows // PAIR
    half = member % PAIR
    scale = logit_scale[0]
    offset = logit_bias[0]

    wide_txt = txt_emb.astype(jnp.float32)
    inv_txt = lax.rsqrt(jnp.sum(wide_txt * wide_txt, axis=1, keepdims=True) + EPSILON)
    unit_txt = wide_txt * inv_txt
    z_txt = unit_txt.astype(jnp.bfloat16)
    pair_txt = jnp.concatenate([z_txt, to_partner(z_txt)], axis=0)
    visitors = [pair_txt] + [passed_along(pair_txt, "dp", k) for k in range(1, STEPS)]

    local_proj = lax.dot_general(
        w_proj, img_feat, (((0,), (1,)), ((), ())), preferred_element_type=jnp.float32
    ).astype(jnp.bfloat16)
    halves = jnp.stack([local_proj[:, h * half_rows : (h + 1) * half_rows] for h in range(PAIR)])
    halves = jnp.broadcast_to(halves[None], (members // PAIR,) + halves.shape)
    projected = swap(halves.reshape(members, width, half_rows), "emb").reshape(features, half_rows)
    wide_img = projected.astype(jnp.float32)
    inv_img = lax.rsqrt(jnp.sum(wide_img * wide_img, axis=0, keepdims=True) + EPSILON)
    unit_img = wide_img * inv_img
    z_img = unit_img.astype(jnp.bfloat16)

    texts = jnp.concatenate(visitors, axis=0)
    cosines = jnp.dot(texts, z_img, preferred_element_type=jnp.float32)
    text_index = lax.broadcasted_iota(jnp.int32, cosines.shape, 0)
    image_index = lax.broadcasted_iota(jnp.int32, cosines.shape, 1) + half * half_rows
    partners = (image_index == (member ^ 1) * text_rows + text_index - text_rows) & (
        (text_index >= text_rows) & (text_index < PAIR * text_rows)
    )
    own = (image_index == member * text_rows + text_index) & (text_index < text_rows)
    signs = jnp.where(own | partners, 1.0, -1.0)
    pair_grad = (-signs * jax.nn.sigmoid(-signs * (scale * cosines + offset))).astype(jnp.bfloat16)
    inner_img = jnp.sum(pair_grad.astype(jnp.float32) * cosines, axis=0, keepdims=True)

    txt_terms = scale * lax.dot_general(
        pair_grad, z_img, (((1,), (1,)), ((), ())), preferred_element_type=jnp.float32
    )
    txt_terms = txt_terms.reshape(STEPS, PAIR, text_rows, features)
    other_terms = to_partner(txt_terms[:, 1].astype(jnp.bfloat16))

    grad_img = lax.dot_general(
        texts, pair_grad, (((0,), (0,)), ((), ())), preferred_element_type=jnp.float32
    )
    grad_proj = (scale * inv_img) * (grad_img - unit_img * inner_img)
    parts = grad_proj.astype(jnp.bfloat16).reshape(members, width, half_rows)
    parts = swap(parts, "emb").reshape(members // PAIR, PAIR, width, half_rows)
    grad_part = summed(parts).astype(jnp.bfloat16)
    grad_part, other_terms = lax.optimization_barrier((grad_part, other_terms))
    grad_part = jnp.concatenate([grad_part[h] for h in range(PAIR)], axis=1)
    local_weight = jnp.dot(grad_part, img_feat, preferred_element_type=jnp.float32)

    txt_terms = txt_terms[:, 0] + other_terms.astype(jnp.float32)
    sent = [passed_along(txt_terms[k].astype(jnp.bfloat16), "dp", -k) for k in range(1, STEPS)]
    d_weight, sent = sum_over_dp(local_weight, sent)

    grad_txt = txt_terms[0]
    for term in sent:
        grad_txt = grad_txt + term.astype(jnp.float32)
    inner_txt = jnp.sum(unit_txt * grad_txt, axis=1, keepdims=True)
    d_text = inv_txt * (grad_txt - unit_txt * inner_txt)
    return (d_weight, d_text)


def solution(mesh):
    in_specs = (P("dp", None), P(None, "emb"), P(("dp", "emb"), None), P(), P())
    out_specs = (P(None, "emb"), P(("dp", "emb"), None))
    return jax.shard_map(local, mesh=mesh, in_specs=in_specs, out_specs=out_specs, check_vma=False)
```

```python
import jax
import jax.numpy as jnp
from jax import lax
from jax.sharding import PartitionSpec as P

STEPS = 3
EPSILON = 1e-06
LANES = 128
ROWS = 8


def passed_along(array, axis, by):
    count = lax.axis_size(axis)
    return lax.ppermute(array, axis, [(i, (i + by) % count) for i in range(count)])


def dp_groups(count):
    z_len = count // 4
    index = lambda hi, z, core: (hi * z_len + z) * 2 + core
    near = [
        [index(hi, z + dz, c) for hi in range(2) for dz in range(2) for c in range(2)]
        for z in range(0, z_len, 2)
    ]
    far = [list(members) for members in zip(*near)]
    return near, far


def swap(parts, axis, groups=None):
    return lax.all_to_all(parts, axis, 0, 0, axis_index_groups=groups)


def gathered(part, count, axis, groups=None):
    return swap(jnp.broadcast_to(part[None], (count,) + part.shape), axis, groups)


def summed(parts):
    return jnp.sum(parts.astype(jnp.float32), axis=0)


def sum_over_dp(grad_t):
    width, features = grad_t.shape
    tiles = features // LANES
    near, far = dp_groups(lax.axis_size("dp"))
    count = len(near[0])
    share = -(-tiles * width // (count * ROWS)) * ROWS
    rows = jnp.concatenate(
        [grad_t[:, LANES * t : LANES * (t + 1)] for t in range(tiles)], axis=0
    ).astype(jnp.bfloat16)
    rows = jnp.pad(rows, ((0, count * share - tiles * width), (0, 0)))
    part = summed(swap(rows.reshape(count, share, LANES), "dp", near)).astype(jnp.bfloat16)
    total = summed(lax.all_gather(part, "dp", axis=0, axis_index_groups=far)).astype(jnp.bfloat16)
    whole = gathered(total, count, "dp", near).reshape(count * share, LANES)[: tiles * width]
    whole = whole.astype(jnp.float32).reshape(tiles, width, LANES)
    return jnp.swapaxes(whole, 1, 2).reshape(features, width)


def local(img_feat, w_proj, txt_emb, logit_scale, logit_bias):
    image_rows, features = img_feat.shape
    text_rows = txt_emb.shape[0]
    width = w_proj.shape[1]
    members = lax.axis_size("emb")
    member = lax.axis_index("emb")
    scale = logit_scale[0]
    offset = logit_bias[0]

    wide_txt = txt_emb.astype(jnp.float32)
    inv_txt = lax.rsqrt(jnp.sum(wide_txt * wide_txt, axis=1, keepdims=True) + EPSILON)
    unit_txt = wide_txt * inv_txt
    z_txt = unit_txt.astype(jnp.bfloat16)
    visitors = [z_txt] + [passed_along(z_txt, "dp", k) for k in range(1, STEPS)]

    local_proj = lax.dot_general(
        w_proj, img_feat, (((0,), (1,)), ((), ())), preferred_element_type=jnp.float32
    ).astype(jnp.bfloat16)
    projected = gathered(local_proj, members, "emb").reshape(features, image_rows)
    wide_img = projected.astype(jnp.float32)
    inv_img = lax.rsqrt(jnp.sum(wide_img * wide_img, axis=0, keepdims=True) + EPSILON)
    unit_img = wide_img * inv_img
    z_img = unit_img.astype(jnp.bfloat16)

    texts = jnp.concatenate(visitors, axis=0)
    cosines = jnp.dot(texts, z_img, preferred_element_type=jnp.float32)
    text_index = lax.broadcasted_iota(jnp.int32, cosines.shape, 0)
    image_index = lax.broadcasted_iota(jnp.int32, cosines.shape, 1)
    own = (text_index < text_rows) & (image_index == member * text_rows + text_index)
    signs = jnp.where(own, 1.0, -1.0)
    pair_grad = (-signs * jax.nn.sigmoid(-signs * (scale * cosines + offset))).astype(jnp.bfloat16)
    inner_img = jnp.sum(pair_grad.astype(jnp.float32) * cosines, axis=0, keepdims=True)

    txt_terms = scale * lax.dot_general(
        pair_grad, z_img, (((1,), (1,)), ((), ())), preferred_element_type=jnp.float32
    )
    sent = [
        passed_along(txt_terms[k * text_rows : (k + 1) * text_rows].astype(jnp.bfloat16), "dp", -k)
        for k in range(1, STEPS)
    ]

    grad_img = lax.dot_general(
        texts, pair_grad, (((0,), (0,)), ((), ())), preferred_element_type=jnp.float32
    )
    grad_proj = (scale * inv_img) * (grad_img - unit_img * inner_img)
    parts = grad_proj.astype(jnp.bfloat16).reshape(members, width, image_rows)
    grad_part = summed(swap(parts, "emb")).astype(jnp.bfloat16)
    grad_part, sent = lax.optimization_barrier((grad_part, sent))
    local_weight = jnp.dot(grad_part, img_feat, preferred_element_type=jnp.float32)
    d_weight = sum_over_dp(local_weight)

    grad_txt = txt_terms[:text_rows]
    for term in sent:
        grad_txt = grad_txt + term.astype(jnp.float32)
    inner_txt = jnp.sum(unit_txt * grad_txt, axis=1, keepdims=True)
    d_text = inv_txt * (grad_txt - unit_txt * inner_txt)
    return (d_weight, d_text)


def solution(mesh):
    in_specs = (P("dp", None), P(None, "emb"), P(("dp", "emb"), None), P(), P())
    out_specs = (P(None, "emb"), P(("dp", "emb"), None))
    return jax.shard_map(local, mesh=mesh, in_specs=in_specs, out_specs=out_specs, check_vma=False)
```

```python
import jax
import jax.numpy as jnp
from jax import lax
from jax.sharding import PartitionSpec as P

STEPS = 3
EPSILON = 1e-06
LANES = 128
ROWS = 8
PAIR = 2


def passed_along(array, axis, by):
    count = lax.axis_size(axis)
    return lax.ppermute(array, axis, [(i, (i + by) % count) for i in range(count)])


def to_partner(array):
    return lax.ppermute(array, "emb", [(i, i ^ 1) for i in range(lax.axis_size("emb"))])


def dp_groups(count):
    z_len = count // 4
    index = lambda hi, z, core: (hi * z_len + z) * 2 + core
    near = [
        [index(hi, z + dz, c) for hi in range(2) for dz in range(2) for c in range(2)]
        for z in range(0, z_len, 2)
    ]
    far = [list(members) for members in zip(*near)]
    return near, far


def swap(parts, axis, groups=None):
    return lax.all_to_all(parts, axis, 0, 0, axis_index_groups=groups)


def gathered(part, count, axis, groups=None):
    return swap(jnp.broadcast_to(part[None], (count,) + part.shape), axis, groups)


def summed(parts):
    return jnp.sum(parts.astype(jnp.float32), axis=0)


def sum_over_dp(grad_t, early):
    width, features = grad_t.shape
    tiles = features // LANES
    near, far = dp_groups(lax.axis_size("dp"))
    count = len(near[0])
    share = -(-tiles * width // (count * ROWS)) * ROWS
    rows = jnp.concatenate(
        [grad_t[:, LANES * t : LANES * (t + 1)] for t in range(tiles)], axis=0
    ).astype(jnp.bfloat16)
    rows = jnp.pad(rows, ((0, count * share - tiles * width), (0, 0)))
    part = summed(swap(rows.reshape(count, share, LANES), "dp", near)).astype(jnp.bfloat16)
    part, early = lax.optimization_barrier((part, early))
    total = summed(lax.all_gather(part, "dp", axis=0, axis_index_groups=far)).astype(jnp.bfloat16)
    whole = gathered(total, count, "dp", near).reshape(count * share, LANES)[: tiles * width]
    whole = whole.astype(jnp.float32).reshape(tiles, width, LANES)
    return jnp.swapaxes(whole, 1, 2).reshape(features, width), early


def local(img_feat, w_proj, txt_emb, logit_scale, logit_bias):
    image_rows, features = img_feat.shape
    text_rows = txt_emb.shape[0]
    width = w_proj.shape[1]
    members = lax.axis_size("emb")
    member = lax.axis_index("emb")
    half_rows = image_rows // PAIR
    half = member % PAIR
    scale = logit_scale[0]
    offset = logit_bias[0]

    wide_txt = txt_emb.astype(jnp.float32)
    inv_txt = lax.rsqrt(jnp.sum(wide_txt * wide_txt, axis=1, keepdims=True) + EPSILON)
    unit_txt = wide_txt * inv_txt
    z_txt = unit_txt.astype(jnp.bfloat16)
    pair_txt = jnp.concatenate([z_txt, to_partner(z_txt)], axis=0)

    local_proj = lax.dot_general(
        w_proj, img_feat, (((0,), (1,)), ((), ())), preferred_element_type=jnp.float32
    ).astype(jnp.bfloat16)
    halves = jnp.stack([local_proj[:, h * half_rows : (h + 1) * half_rows] for h in range(PAIR)])
    halves = jnp.broadcast_to(halves[None], (members // PAIR,) + halves.shape)
    halves, pair_txt = lax.optimization_barrier((halves, pair_txt))
    visitors = [pair_txt] + [passed_along(pair_txt, "dp", k) for k in range(1, STEPS)]
    projected = swap(halves.reshape(members, width, half_rows), "emb").reshape(features, half_rows)
    wide_img = projected.astype(jnp.float32)
    inv_img = lax.rsqrt(jnp.sum(wide_img * wide_img, axis=0, keepdims=True) + EPSILON)
    unit_img = wide_img * inv_img
    z_img = unit_img.astype(jnp.bfloat16)

    texts = lax.optimization_barrier(jnp.concatenate(visitors, axis=0))
    cosines = jnp.dot(texts, z_img, preferred_element_type=jnp.float32)
    text_index = lax.broadcasted_iota(jnp.int32, cosines.shape, 0)
    image_index = lax.broadcasted_iota(jnp.int32, cosines.shape, 1) + half * half_rows
    partners = (image_index == (member ^ 1) * text_rows + text_index - text_rows) & (
        (text_index >= text_rows) & (text_index < PAIR * text_rows)
    )
    own = (image_index == member * text_rows + text_index) & (text_index < text_rows)
    signs = jnp.where(own | partners, 1.0, -1.0)
    pair_grad = (-signs * jax.nn.sigmoid(-signs * (scale * cosines + offset))).astype(jnp.bfloat16)
    inner_img = jnp.sum(pair_grad.astype(jnp.float32) * cosines, axis=0, keepdims=True)

    txt_terms = scale * lax.dot_general(
        pair_grad, z_img, (((1,), (1,)), ((), ())), preferred_element_type=jnp.float32
    )
    txt_terms = txt_terms.reshape(STEPS, PAIR, text_rows, features)
    other_terms = to_partner(txt_terms[:, 1].astype(jnp.bfloat16))

    grad_img = lax.dot_general(
        texts, pair_grad, (((0,), (0,)), ((), ())), preferred_element_type=jnp.float32
    )
    grad_proj = (scale * inv_img) * (grad_img - unit_img * inner_img)
    parts = grad_proj.astype(jnp.bfloat16).reshape(members, width, half_rows)
    parts = swap(parts, "emb").reshape(members // PAIR, PAIR, width, half_rows)
    grad_part = summed(parts).astype(jnp.bfloat16)
    grad_part = jnp.concatenate([grad_part[h] for h in range(PAIR)], axis=1)
    local_weight = jnp.dot(grad_part, img_feat, preferred_element_type=jnp.float32)

    txt_terms = txt_terms[:, 0] + other_terms.astype(jnp.float32)
    sent = [passed_along(txt_terms[k].astype(jnp.bfloat16), "dp", -k) for k in range(1, STEPS)]
    d_weight, sent = sum_over_dp(local_weight, sent)

    grad_txt = txt_terms[0]
    for term in sent:
        grad_txt = grad_txt + term.astype(jnp.float32)
    inner_txt = jnp.sum(unit_txt * grad_txt, axis=1, keepdims=True)
    d_text = inv_txt * (grad_txt - unit_txt * inner_txt)
    return (d_weight, d_text)


def solution(mesh):
    in_specs = (P("dp", None), P(None, "emb"), P(("dp", "emb"), None), P(), P())
    out_specs = (P(None, "emb"), P(("dp", "emb"), None))
    return jax.shard_map(local, mesh=mesh, in_specs=in_specs, out_specs=out_specs, check_vma=False)
```

```python
import jax
import jax.numpy as jnp
from jax import lax
from jax.sharding import PartitionSpec as P

STEPS = 3
EPSILON = 1e-06
LANES = 128
ROWS = 8
PAIR = 2


def passed_along(array, axis, by):
    count = lax.axis_size(axis)
    return lax.ppermute(array, axis, [(i, (i + by) % count) for i in range(count)])


def to_partner(array):
    return lax.ppermute(array, "emb", [(i, i ^ 1) for i in range(lax.axis_size("emb"))])


def dp_groups(count):
    z_len = count // 4
    index = lambda hi, z, core: (hi * z_len + z) * 2 + core
    near = [
        [index(hi, z + dz, c) for hi in range(2) for dz in range(2) for c in range(2)]
        for z in range(0, z_len, 2)
    ]
    far = [list(members) for members in zip(*near)]
    return near, far


def swap(parts, axis, groups=None):
    return lax.all_to_all(parts, axis, 0, 0, axis_index_groups=groups)


def gathered(part, count, axis, groups=None):
    return swap(jnp.broadcast_to(part[None], (count,) + part.shape), axis, groups)


def summed(parts):
    return jnp.sum(parts.astype(jnp.float32), axis=0)


def sum_over_dp(grad_t, early):
    width, features = grad_t.shape
    tiles = features // LANES
    near, far = dp_groups(lax.axis_size("dp"))
    count = len(near[0])
    share = -(-tiles * width // (count * ROWS)) * ROWS
    rows = jnp.concatenate(
        [grad_t[:, LANES * t : LANES * (t + 1)] for t in range(tiles)], axis=0
    ).astype(jnp.bfloat16)
    rows = jnp.pad(rows, ((0, count * share - tiles * width), (0, 0)))
    part = summed(swap(rows.reshape(count, share, LANES), "dp", near)).astype(jnp.bfloat16)
    total = summed(lax.all_gather(part, "dp", axis=0, axis_index_groups=far)).astype(jnp.bfloat16)
    total, early = lax.optimization_barrier((total, early))
    whole = gathered(total, count, "dp", near).reshape(count * share, LANES)[: tiles * width]
    whole = whole.astype(jnp.float32).reshape(tiles, width, LANES)
    return jnp.swapaxes(whole, 1, 2).reshape(features, width), early


def unit_columns(values):
    wide = values.astype(jnp.float32)
    inverse = lax.rsqrt(jnp.sum(wide * wide, axis=0, keepdims=True) + EPSILON)
    return wide * inverse, inverse


def unit_rows(values):
    wide = values.astype(jnp.float32)
    inverse = lax.rsqrt(jnp.sum(wide * wide, axis=1, keepdims=True) + EPSILON)
    return wide * inverse, inverse


def local(img_feat, w_proj, txt_emb, logit_scale, logit_bias):
    image_rows, features = img_feat.shape
    text_rows = txt_emb.shape[0]
    width = w_proj.shape[1]
    members = lax.axis_size("emb")
    member = lax.axis_index("emb")
    half_rows = image_rows // PAIR
    first_row = (member % PAIR) * half_rows
    scale = logit_scale[0]
    offset = logit_bias[0]

    def slopes(texts, images, matches):
        cosines = jnp.dot(texts, images, preferred_element_type=jnp.float32)
        text = lax.broadcasted_iota(jnp.int32, cosines.shape, 0)
        image = lax.broadcasted_iota(jnp.int32, cosines.shape, 1)
        signs = jnp.where(matches(text, image), 1.0, -1.0)
        grads = -signs * jax.nn.sigmoid(-signs * (scale * cosines + offset))
        return cosines, grads.astype(jnp.bfloat16)

    partner_txt = to_partner(txt_emb)
    local_proj = lax.dot_general(
        w_proj, img_feat, (((0,), (1,)), ((), ())), preferred_element_type=jnp.float32
    ).astype(jnp.bfloat16)
    copies = jnp.broadcast_to(local_proj[None], (members,) + local_proj.shape)
    copies, partner_txt = lax.optimization_barrier((copies, partner_txt))
    unit_txt, inv_txt = unit_rows(txt_emb)
    pair_txt = jnp.concatenate([unit_txt, unit_rows(partner_txt)[0]], axis=0).astype(jnp.bfloat16)
    visitors = [pair_txt] + [passed_along(pair_txt, "dp", k) for k in range(1, STEPS)]
    projected = swap(copies, "emb").reshape(features, image_rows)

    mine = lax.dynamic_slice_in_dim(projected, first_row, half_rows, 1)
    unit_img, inv_img = unit_columns(mine)
    texts = lax.optimization_barrier(jnp.concatenate(visitors, axis=0))

    def pair_matches(text, image):
        row = image + first_row
        own = (text < text_rows) & (row == member * text_rows + text)
        other = (text >= text_rows) & (text < PAIR * text_rows)
        return own | (other & (row == (member ^ 1) * text_rows + text - text_rows))

    cosines, pair_grad = slopes(texts, unit_img.astype(jnp.bfloat16), pair_matches)
    inner_img = jnp.sum(pair_grad.astype(jnp.float32) * cosines, axis=0, keepdims=True)
    grad_img = lax.dot_general(
        texts, pair_grad, (((0,), (0,)), ((), ())), preferred_element_type=jnp.float32
    )
    grad_proj = (scale * inv_img) * (grad_img - unit_img * inner_img)
    parts = grad_proj.astype(jnp.bfloat16).reshape(members, width, half_rows)
    parts = swap(parts, "emb").reshape(members // PAIR, PAIR, width, half_rows)
    grad_part = summed(parts).astype(jnp.bfloat16)
    grad_part = jnp.concatenate([grad_part[h] for h in range(PAIR)], axis=1)
    local_weight = jnp.dot(grad_part, img_feat, preferred_element_type=jnp.float32)

    own_texts = jnp.concatenate([visitor[:text_rows] for visitor in visitors], axis=0)
    z_img = unit_columns(projected)[0].astype(jnp.bfloat16)
    own_grad = slopes(
        own_texts,
        z_img,
        lambda text, image: (text < text_rows) & (image == member * text_rows + text),
    )[1]
    txt_terms = scale * lax.dot_general(
        own_grad, z_img, (((1,), (1,)), ((), ())), preferred_element_type=jnp.float32
    )
    sent = [
        passed_along(txt_terms[k * text_rows : (k + 1) * text_rows].astype(jnp.bfloat16), "dp", -k)
        for k in range(1, STEPS)
    ]
    d_weight, sent = sum_over_dp(local_weight, sent)

    grad_txt = txt_terms[:text_rows]
    for term in sent:
        grad_txt = grad_txt + term.astype(jnp.float32)
    inner_txt = jnp.sum(unit_txt * grad_txt, axis=1, keepdims=True)
    d_text = inv_txt * (grad_txt - unit_txt * inner_txt)
    return (d_weight, d_text)


def solution(mesh):
    in_specs = (P("dp", None), P(None, "emb"), P(("dp", "emb"), None), P(), P())
    out_specs = (P(None, "emb"), P(("dp", "emb"), None))
    return jax.shard_map(local, mesh=mesh, in_specs=in_specs, out_specs=out_specs, check_vma=False)
```

```python
import jax
import jax.numpy as jnp
from jax import lax
from jax.sharding import PartitionSpec as P

STEPS = 3
EPSILON = 1e-06
LANES = 128
ROWS = 8
PAIR = 2


def passed_along(array, axis, by):
    count = lax.axis_size(axis)
    return lax.ppermute(array, axis, [(i, (i + by) % count) for i in range(count)])


def to_partner(array):
    return lax.ppermute(array, "emb", [(i, i ^ 1) for i in range(lax.axis_size("emb"))])


def dp_groups(count):
    z_len = count // 4
    index = lambda hi, z, core: (hi * z_len + z) * 2 + core
    near = [
        [index(hi, z + dz, c) for hi in range(2) for dz in range(2) for c in range(2)]
        for z in range(0, z_len, 2)
    ]
    far = [list(members) for members in zip(*near)]
    return near, far


def swap(parts, axis, groups=None):
    return lax.all_to_all(parts, axis, 0, 0, axis_index_groups=groups)


def gathered(part, count, axis, groups=None):
    return swap(jnp.broadcast_to(part[None], (count,) + part.shape), axis, groups)


def summed(parts):
    return jnp.sum(parts.astype(jnp.float32), axis=0)


def sum_over_dp(grad_t, early):
    width, features = grad_t.shape
    tiles = features // LANES
    near, far = dp_groups(lax.axis_size("dp"))
    count = len(near[0])
    share = -(-tiles * width // (count * ROWS)) * ROWS
    rows = jnp.concatenate(
        [grad_t[:, LANES * t : LANES * (t + 1)] for t in range(tiles)], axis=0
    ).astype(jnp.bfloat16)
    rows = jnp.pad(rows, ((0, count * share - tiles * width), (0, 0)))
    part = summed(swap(rows.reshape(count, share, LANES), "dp", near)).astype(jnp.bfloat16)
    total = summed(lax.all_gather(part, "dp", axis=0, axis_index_groups=far)).astype(jnp.bfloat16)
    total, early = lax.optimization_barrier((total, early))
    whole = gathered(total, count, "dp", near).reshape(count * share, LANES)[: tiles * width]
    whole = whole.astype(jnp.float32).reshape(tiles, width, LANES)
    return jnp.swapaxes(whole, 1, 2).reshape(features, width), early


def unit_columns(values):
    wide = values.astype(jnp.float32)
    inverse = lax.rsqrt(jnp.sum(wide * wide, axis=0, keepdims=True) + EPSILON)
    return wide * inverse, inverse


def unit_rows(values):
    wide = values.astype(jnp.float32)
    inverse = lax.rsqrt(jnp.sum(wide * wide, axis=1, keepdims=True) + EPSILON)
    return wide * inverse, inverse


def local(img_feat, w_proj, txt_emb, logit_scale, logit_bias):
    image_rows, features = img_feat.shape
    text_rows = txt_emb.shape[0]
    width = w_proj.shape[1]
    members = lax.axis_size("emb")
    member = lax.axis_index("emb")
    half_rows = image_rows // PAIR
    first_row = (member % PAIR) * half_rows
    scale = logit_scale[0]
    offset = logit_bias[0]

    def slopes(texts, images, matches):
        cosines = jnp.dot(texts, images, preferred_element_type=jnp.float32)
        text = lax.broadcasted_iota(jnp.int32, cosines.shape, 0)
        image = lax.broadcasted_iota(jnp.int32, cosines.shape, 1)
        signs = jnp.where(matches(text, image), 1.0, -1.0)
        grads = -signs * jax.nn.sigmoid(-signs * (scale * cosines + offset))
        return cosines, grads.astype(jnp.bfloat16)

    partner_txt = to_partner(txt_emb)
    local_proj = lax.dot_general(
        w_proj, img_feat, (((0,), (1,)), ((), ())), preferred_element_type=jnp.float32
    ).astype(jnp.bfloat16)
    copies = jnp.broadcast_to(local_proj[None], (members,) + local_proj.shape)
    copies, txt_emb, partner_txt = lax.optimization_barrier((copies, txt_emb, partner_txt))
    unit_txt, inv_txt = unit_rows(txt_emb)
    pair_txt = jnp.concatenate([unit_txt, unit_rows(partner_txt)[0]], axis=0).astype(jnp.bfloat16)
    visitors = [pair_txt] + [passed_along(pair_txt, "dp", k) for k in range(1, STEPS)]
    projected = swap(copies, "emb").reshape(features, image_rows)

    mine = lax.dynamic_slice_in_dim(projected, first_row, half_rows, 1)
    unit_img, inv_img = unit_columns(mine)
    texts = lax.optimization_barrier(jnp.concatenate(visitors, axis=0))

    def pair_matches(text, image):
        row = image + first_row
        own = (text < text_rows) & (row == member * text_rows + text)
        other = (text >= text_rows) & (text < PAIR * text_rows)
        return own | (other & (row == (member ^ 1) * text_rows + text - text_rows))

    cosines, pair_grad = slopes(texts, unit_img.astype(jnp.bfloat16), pair_matches)
    inner_img = jnp.sum(pair_grad.astype(jnp.float32) * cosines, axis=0, keepdims=True)
    grad_img = lax.dot_general(
        texts, pair_grad, (((0,), (0,)), ((), ())), preferred_element_type=jnp.float32
    )
    grad_proj = (scale * inv_img) * (grad_img - unit_img * inner_img)
    parts = grad_proj.astype(jnp.bfloat16).reshape(members, width, half_rows)
    parts = swap(parts, "emb").reshape(members // PAIR, PAIR, width, half_rows)
    grad_part = summed(parts).astype(jnp.bfloat16)
    own_texts = jnp.concatenate([visitor[:text_rows] for visitor in visitors], axis=0)
    z_img = unit_columns(projected)[0].astype(jnp.bfloat16)
    own_grad = slopes(
        own_texts,
        z_img,
        lambda text, image: (text < text_rows) & (image == member * text_rows + text),
    )[1]
    txt_terms = scale * lax.dot_general(
        own_grad, z_img, (((1,), (1,)), ((), ())), preferred_element_type=jnp.float32
    )
    grad_part, txt_terms = lax.optimization_barrier((grad_part, txt_terms))
    grad_part = jnp.concatenate([grad_part[h] for h in range(PAIR)], axis=1)
    local_weight = jnp.dot(grad_part, img_feat, preferred_element_type=jnp.float32)

    sent = [
        passed_along(txt_terms[k * text_rows : (k + 1) * text_rows].astype(jnp.bfloat16), "dp", -k)
        for k in range(1, STEPS)
    ]
    d_weight, sent = sum_over_dp(local_weight, sent)

    grad_txt = txt_terms[:text_rows]
    for term in sent:
        grad_txt = grad_txt + term.astype(jnp.float32)
    inner_txt = jnp.sum(unit_txt * grad_txt, axis=1, keepdims=True)
    d_text = inv_txt * (grad_txt - unit_txt * inner_txt)
    return (d_weight, d_text)


def solution(mesh):
    in_specs = (P("dp", None), P(None, "emb"), P(("dp", "emb"), None), P(), P())
    out_specs = (P(None, "emb"), P(("dp", "emb"), None))
    return jax.shard_map(local, mesh=mesh, in_specs=in_specs, out_specs=out_specs, check_vma=False)
```

```python
import jax
import jax.numpy as jnp
from jax import lax
from jax.sharding import PartitionSpec as P

STEPS = 3
EPSILON = 1e-06
LANES = 128
ROWS = 8
PAIR = 2


def passed_along(array, axis, by):
    count = lax.axis_size(axis)
    return lax.ppermute(array, axis, [(i, (i + by) % count) for i in range(count)])


def to_partner(array):
    return lax.ppermute(array, "emb", [(i, i ^ 1) for i in range(lax.axis_size("emb"))])


def dp_groups(count):
    z_len = count // 4
    index = lambda hi, z, core: (hi * z_len + z) * 2 + core
    near = [
        [index(hi, z + dz, c) for hi in range(2) for dz in range(2) for c in range(2)]
        for z in range(0, z_len, 2)
    ]
    far = [list(members) for members in zip(*near)]
    return near, far


def swap(parts, axis, groups=None):
    return lax.all_to_all(parts, axis, 0, 0, axis_index_groups=groups)


def gathered(part, count, axis, groups=None):
    return swap(jnp.broadcast_to(part[None], (count,) + part.shape), axis, groups)


def repeated(blocks, times):
    copies = jnp.broadcast_to(blocks[None], (times,) + blocks.shape)
    return copies.reshape((times * blocks.shape[0],) + blocks.shape[1:])


def summed(parts):
    return jnp.sum(parts.astype(jnp.float32), axis=0)


def sum_over_dp(grad_t, early):
    width, features = grad_t.shape
    tiles = features // LANES
    near, far = dp_groups(lax.axis_size("dp"))
    count = len(near[0])
    share = -(-tiles * width // (count * ROWS)) * ROWS
    rows = jnp.concatenate(
        [grad_t[:, LANES * t : LANES * (t + 1)] for t in range(tiles)], axis=0
    ).astype(jnp.bfloat16)
    rows = jnp.pad(rows, ((0, count * share - tiles * width), (0, 0)))
    part = summed(swap(rows.reshape(count, share, LANES), "dp", near)).astype(jnp.bfloat16)
    total = summed(lax.all_gather(part, "dp", axis=0, axis_index_groups=far)).astype(jnp.bfloat16)
    total, early = lax.optimization_barrier((total, early))
    whole = gathered(total, count, "dp", near).reshape(count * share, LANES)[: tiles * width]
    whole = whole.astype(jnp.float32).reshape(tiles, width, LANES)
    return jnp.swapaxes(whole, 1, 2).reshape(features, width), early


def unit_columns(values):
    wide = values.astype(jnp.float32)
    inverse = lax.rsqrt(jnp.sum(wide * wide, axis=0, keepdims=True) + EPSILON)
    return wide * inverse, inverse


def unit_rows(values):
    wide = values.astype(jnp.float32)
    inverse = lax.rsqrt(jnp.sum(wide * wide, axis=1, keepdims=True) + EPSILON)
    return wide * inverse, inverse


def local(img_feat, w_proj, txt_emb, logit_scale, logit_bias):
    image_rows, features = img_feat.shape
    text_rows = txt_emb.shape[0]
    width = w_proj.shape[1]
    members = lax.axis_size("emb")
    member = lax.axis_index("emb")
    half_rows = image_rows // PAIR
    first_row = (member % PAIR) * half_rows
    scale = logit_scale[0]
    offset = logit_bias[0]

    def slopes(texts, images, matches):
        cosines = jnp.dot(texts, images, preferred_element_type=jnp.float32)
        text = lax.broadcasted_iota(jnp.int32, cosines.shape, 0)
        image = lax.broadcasted_iota(jnp.int32, cosines.shape, 1)
        signs = jnp.where(matches(text, image), 1.0, -1.0)
        grads = -signs * jax.nn.sigmoid(-signs * (scale * cosines + offset))
        return cosines, grads.astype(jnp.bfloat16)

    pair_txt = jnp.concatenate([txt_emb, to_partner(txt_emb)], axis=0)
    local_proj = lax.dot_general(
        w_proj, img_feat, (((0,), (1,)), ((), ())), preferred_element_type=jnp.float32
    ).astype(jnp.bfloat16)
    halves = [local_proj[:, h * half_rows : (h + 1) * half_rows] for h in range(PAIR)]
    wanted = repeated(jnp.stack(halves), members // PAIR)
    others = repeated(jnp.stack(halves[::-1]), members // PAIR)
    wanted, pair_txt = lax.optimization_barrier((wanted, pair_txt))
    visitors = [pair_txt] + [passed_along(pair_txt, "dp", k) for k in range(1, STEPS)]
    mine = swap(wanted, "emb").reshape(features, half_rows)

    unit_img, inv_img = unit_columns(mine)
    z_img = unit_img.astype(jnp.bfloat16)
    texts = unit_rows(jnp.concatenate(visitors, axis=0))[0].astype(jnp.bfloat16)

    def pair_matches(text, image):
        row = image + first_row
        own = (text < text_rows) & (row == member * text_rows + text)
        other = (text >= text_rows) & (text < PAIR * text_rows)
        return own | (other & (row == (member ^ 1) * text_rows + text - text_rows))

    cosines, pair_grad = slopes(texts, z_img, pair_matches)
    inner_img = jnp.sum(pair_grad.astype(jnp.float32) * cosines, axis=0, keepdims=True)
    grad_img = lax.dot_general(
        texts, pair_grad, (((0,), (0,)), ((), ())), preferred_element_type=jnp.float32
    )
    grad_proj = (scale * inv_img) * (grad_img - unit_img * inner_img)
    parts = grad_proj.astype(jnp.bfloat16).reshape(members, width, half_rows)
    parts, others = lax.optimization_barrier((parts, others))
    parts = swap(parts, "emb").reshape(members // PAIR, PAIR, width, half_rows)
    grad_part = summed(parts).astype(jnp.bfloat16)
    grad_part = jnp.concatenate([grad_part[h] for h in range(PAIR)], axis=1)
    local_weight = jnp.dot(grad_part, img_feat, preferred_element_type=jnp.float32)

    z_other = unit_columns(swap(others, "emb").reshape(features, half_rows))[0].astype(jnp.bfloat16)
    starts = [k * PAIR * text_rows for k in range(STEPS)]
    own_rows = lambda array: jnp.concatenate([array[i : i + text_rows] for i in starts], axis=0)
    other_row = half_rows - first_row
    other_grad = slopes(
        own_rows(texts),
        z_other,
        lambda text, image: (text < text_rows) & (image + other_row == member * text_rows + text),
    )[1]
    over_images = lambda grads, images: lax.dot_general(
        grads, images, (((1,), (1,)), ((), ())), preferred_element_type=jnp.float32
    )
    txt_terms = scale * (over_images(own_rows(pair_grad), z_img) + over_images(other_grad, z_other))
    sent = [
        passed_along(txt_terms[k * text_rows : (k + 1) * text_rows].astype(jnp.bfloat16), "dp", -k)
        for k in range(1, STEPS)
    ]
    unit_txt, inv_txt = unit_rows(txt_emb)
    d_weight, sent = sum_over_dp(local_weight, sent)

    grad_txt = txt_terms[:text_rows]
    for term in sent:
        grad_txt = grad_txt + term.astype(jnp.float32)
    inner_txt = jnp.sum(unit_txt * grad_txt, axis=1, keepdims=True)
    d_text = inv_txt * (grad_txt - unit_txt * inner_txt)
    return (d_weight, d_text)


def solution(mesh):
    in_specs = (P("dp", None), P(None, "emb"), P(("dp", "emb"), None), P(), P())
    out_specs = (P(None, "emb"), P(("dp", "emb"), None))
    return jax.shard_map(local, mesh=mesh, in_specs=in_specs, out_specs=out_specs, check_vma=False)
```

```python
import jax
import jax.numpy as jnp
from jax import lax
from jax.sharding import PartitionSpec as P

STEPS = 3
EPSILON = 1e-06
LANES = 128
ROWS = 8


def passed_along(array, axis, by):
    count = lax.axis_size(axis)
    return lax.ppermute(array, axis, [(i, (i + by) % count) for i in range(count)])


def dp_groups(count):
    z_len = count // 4
    index = lambda hi, z, core: (hi * z_len + z) * 2 + core
    near = [
        [index(hi, z + dz, c) for hi in range(2) for dz in range(2) for c in range(2)]
        for z in range(0, z_len, 2)
    ]
    far = [list(members) for members in zip(*near)]
    return near, far


def swap(parts, axis, groups=None):
    return lax.all_to_all(parts, axis, 0, 0, axis_index_groups=groups)


def gathered(part, count, axis, groups=None):
    return swap(jnp.broadcast_to(part[None], (count,) + part.shape), axis, groups)


def summed(parts):
    return jnp.sum(parts.astype(jnp.float32), axis=0)


def sum_over_dp(grad_t, early):
    width, features = grad_t.shape
    tiles = features // LANES
    near, far = dp_groups(lax.axis_size("dp"))
    count = len(near[0])
    share = -(-tiles * width // (count * ROWS)) * ROWS
    rows = jnp.concatenate(
        [grad_t[:, LANES * t : LANES * (t + 1)] for t in range(tiles)], axis=0
    ).astype(jnp.bfloat16)
    rows = jnp.pad(rows, ((0, count * share - tiles * width), (0, 0)))
    part = summed(swap(rows.reshape(count, share, LANES), "dp", near)).astype(jnp.bfloat16)
    total = summed(lax.all_gather(part, "dp", axis=0, axis_index_groups=far)).astype(jnp.bfloat16)
    total, early = lax.optimization_barrier((total, early))
    whole = gathered(total, count, "dp", near).reshape(count * share, LANES)[: tiles * width]
    whole = whole.astype(jnp.float32).reshape(tiles, width, LANES)
    return jnp.swapaxes(whole, 1, 2).reshape(features, width), early


def local(img_feat, w_proj, txt_emb, logit_scale, logit_bias):
    image_rows, features = img_feat.shape
    text_rows = txt_emb.shape[0]
    width = w_proj.shape[1]
    members = lax.axis_size("emb")
    member = lax.axis_index("emb")
    scale = logit_scale[0]
    offset = logit_bias[0]

    visitors = [txt_emb] + [passed_along(txt_emb, "dp", k) for k in range(1, STEPS)]
    local_proj = lax.dot_general(
        w_proj, img_feat, (((0,), (1,)), ((), ())), preferred_element_type=jnp.float32
    ).astype(jnp.bfloat16)
    copies = jnp.broadcast_to(local_proj[None], (members,) + local_proj.shape)
    copies, visitors = lax.optimization_barrier((copies, visitors))
    projected = swap(copies, "emb").reshape(features, image_rows)

    wide_txt = jnp.concatenate(visitors, axis=0).astype(jnp.float32)
    inverse_txt = lax.rsqrt(jnp.sum(wide_txt * wide_txt, axis=1, keepdims=True) + EPSILON)
    texts = (wide_txt * inverse_txt).astype(jnp.bfloat16)
    inv_txt = inverse_txt[:text_rows]
    unit_txt = txt_emb.astype(jnp.float32) * inv_txt
    wide_img = projected.astype(jnp.float32)
    inv_img = lax.rsqrt(jnp.sum(wide_img * wide_img, axis=0, keepdims=True) + EPSILON)
    unit_img = wide_img * inv_img
    z_img = unit_img.astype(jnp.bfloat16)

    cosines = jnp.dot(texts, z_img, preferred_element_type=jnp.float32)
    text_index = lax.broadcasted_iota(jnp.int32, cosines.shape, 0)
    image_index = lax.broadcasted_iota(jnp.int32, cosines.shape, 1)
    own = (text_index < text_rows) & (image_index == member * text_rows + text_index)
    signs = jnp.where(own, 1.0, -1.0)
    pair_grad = (-signs * jax.nn.sigmoid(-signs * (scale * cosines + offset))).astype(jnp.bfloat16)
    inner_img = jnp.sum(pair_grad.astype(jnp.float32) * cosines, axis=0, keepdims=True)

    txt_terms = scale * lax.dot_general(
        pair_grad, z_img, (((1,), (1,)), ((), ())), preferred_element_type=jnp.float32
    )
    sent = [
        passed_along(txt_terms[k * text_rows : (k + 1) * text_rows].astype(jnp.bfloat16), "dp", -k)
        for k in range(1, STEPS)
    ]

    grad_img = lax.dot_general(
        texts, pair_grad, (((0,), (0,)), ((), ())), preferred_element_type=jnp.float32
    )
    grad_proj = (scale * inv_img) * (grad_img - unit_img * inner_img)
    parts = grad_proj.astype(jnp.bfloat16).reshape(members, width, image_rows)
    grad_part = summed(swap(parts, "emb")).astype(jnp.bfloat16)
    local_weight = jnp.dot(grad_part, img_feat, preferred_element_type=jnp.float32)
    d_weight, sent = sum_over_dp(local_weight, sent)

    grad_txt = txt_terms[:text_rows]
    for term in sent:
        grad_txt = grad_txt + term.astype(jnp.float32)
    inner_txt = jnp.sum(unit_txt * grad_txt, axis=1, keepdims=True)
    d_text = inv_txt * (grad_txt - unit_txt * inner_txt)
    return (d_weight, d_text)


def solution(mesh):
    in_specs = (P("dp", None), P(None, "emb"), P(("dp", "emb"), None), P(), P())
    out_specs = (P(None, "emb"), P(("dp", "emb"), None))
    return jax.shard_map(local, mesh=mesh, in_specs=in_specs, out_specs=out_specs, check_vma=False)
```

```python
import jax
import jax.numpy as jnp
from jax import lax
from jax.sharding import PartitionSpec as P

STEPS = 3
EPSILON = 1e-06
LANES = 128
ROWS = 8
PAIR = 2


def passed_along(array, axis, by):
    count = lax.axis_size(axis)
    return lax.ppermute(array, axis, [(i, (i + by) % count) for i in range(count)])


def to_partner(array):
    return lax.ppermute(array, "emb", [(i, i ^ 1) for i in range(lax.axis_size("emb"))])


def dp_groups(count):
    z_len = count // 4
    index = lambda hi, z, core: (hi * z_len + z) * 2 + core
    near = [
        [index(hi, z + dz, c) for hi in range(2) for dz in range(2) for c in range(2)]
        for z in range(0, z_len, 2)
    ]
    far = [list(members) for members in zip(*near)]
    return near, far


def swap(parts, axis, groups=None):
    return lax.all_to_all(parts, axis, 0, 0, axis_index_groups=groups)


def gathered(part, count, axis, groups=None):
    return swap(jnp.broadcast_to(part[None], (count,) + part.shape), axis, groups)


def summed(parts):
    return jnp.sum(parts.astype(jnp.float32), axis=0)


def sum_over_dp(grad_t, early):
    width, features = grad_t.shape
    tiles = features // LANES
    near, far = dp_groups(lax.axis_size("dp"))
    count = len(near[0])
    share = -(-tiles * width // (count * ROWS)) * ROWS
    rows = jnp.concatenate(
        [grad_t[:, LANES * t : LANES * (t + 1)] for t in range(tiles)], axis=0
    ).astype(jnp.bfloat16)
    rows = jnp.pad(rows, ((0, count * share - tiles * width), (0, 0)))
    part = summed(swap(rows.reshape(count, share, LANES), "dp", near)).astype(jnp.bfloat16)
    total = summed(lax.all_gather(part, "dp", axis=0, axis_index_groups=far)).astype(jnp.bfloat16)
    total, early = lax.optimization_barrier((total, early))
    whole = gathered(total, count, "dp", near).reshape(count * share, LANES)[: tiles * width]
    whole = whole.astype(jnp.float32).reshape(tiles, width, LANES)
    return jnp.swapaxes(whole, 1, 2).reshape(features, width), early


def unit_columns(values):
    wide = values.astype(jnp.float32)
    inverse = lax.rsqrt(jnp.sum(wide * wide, axis=0, keepdims=True) + EPSILON)
    return wide * inverse, inverse


def unit_rows(values):
    wide = values.astype(jnp.float32)
    inverse = lax.rsqrt(jnp.sum(wide * wide, axis=1, keepdims=True) + EPSILON)
    return wide * inverse, inverse


def local(img_feat, w_proj, txt_emb, logit_scale, logit_bias):
    image_rows, features = img_feat.shape
    text_rows = txt_emb.shape[0]
    width = w_proj.shape[1]
    members = lax.axis_size("emb")
    member = lax.axis_index("emb")
    half_rows = image_rows // PAIR
    first_row = (member % PAIR) * half_rows
    scale = logit_scale[0]
    offset = logit_bias[0]

    def slopes(texts, images, matches):
        cosines = jnp.dot(texts, images, preferred_element_type=jnp.float32)
        text = lax.broadcasted_iota(jnp.int32, cosines.shape, 0)
        image = lax.broadcasted_iota(jnp.int32, cosines.shape, 1)
        signs = jnp.where(matches(text, image), 1.0, -1.0)
        grads = -signs * jax.nn.sigmoid(-signs * (scale * cosines + offset))
        return cosines, grads.astype(jnp.bfloat16)

    partner_txt = to_partner(txt_emb)
    local_proj = lax.dot_general(
        w_proj, img_feat, (((0,), (1,)), ((), ())), preferred_element_type=jnp.float32
    ).astype(jnp.bfloat16)
    copies = jnp.broadcast_to(local_proj[None], (members,) + local_proj.shape)
    copies, txt_emb, partner_txt = lax.optimization_barrier((copies, txt_emb, partner_txt))
    unit_txt, inv_txt = unit_rows(txt_emb)
    pair_txt = jnp.concatenate([unit_txt, unit_rows(partner_txt)[0]], axis=0).astype(jnp.bfloat16)
    visitors = [pair_txt] + [passed_along(pair_txt, "dp", k) for k in range(1, STEPS)]
    projected = swap(copies, "emb").reshape(features, image_rows)

    mine = lax.dynamic_slice_in_dim(projected, first_row, half_rows, 1)
    unit_img, inv_img = unit_columns(mine)
    texts = lax.optimization_barrier(jnp.concatenate(visitors, axis=0))

    def pair_matches(text, image):
        row = image + first_row
        own = (text < text_rows) & (row == member * text_rows + text)
        other = (text >= text_rows) & (text < PAIR * text_rows)
        return own | (other & (row == (member ^ 1) * text_rows + text - text_rows))

    z_img = unit_img.astype(jnp.bfloat16)
    cosines, pair_grad = slopes(texts, z_img, pair_matches)
    inner_img = jnp.sum(pair_grad.astype(jnp.float32) * cosines, axis=0, keepdims=True)
    grad_img = lax.dot_general(
        texts, pair_grad, (((0,), (0,)), ((), ())), preferred_element_type=jnp.float32
    )
    grad_proj = (scale * inv_img) * (grad_img - unit_img * inner_img)
    parts = grad_proj.astype(jnp.bfloat16).reshape(members, width, half_rows)
    parts = swap(parts, "emb").reshape(members // PAIR, PAIR, width, half_rows)
    grad_part = summed(parts).astype(jnp.bfloat16)
    grad_part = jnp.concatenate([grad_part[h] for h in range(PAIR)], axis=1)
    local_weight = jnp.dot(grad_part, img_feat, preferred_element_type=jnp.float32)

    own_rows = lambda array: jnp.concatenate(
        [array[k * PAIR * text_rows :][:text_rows] for k in range(STEPS)], axis=0
    )
    over_images = lambda grads, images: lax.dot_general(
        grads, images, (((1,), (1,)), ((), ())), preferred_element_type=jnp.float32
    )
    other_row = half_rows - first_row
    other = lax.dynamic_slice_in_dim(projected, other_row, half_rows, 1)
    z_other = unit_columns(other)[0].astype(jnp.bfloat16)
    other_grad = slopes(
        own_rows(texts),
        z_other,
        lambda text, image: (text < text_rows) & (image + other_row == member * text_rows + text),
    )[1]
    txt_terms = scale * (over_images(own_rows(pair_grad), z_img) + over_images(other_grad, z_other))
    sent = [
        passed_along(txt_terms[k * text_rows : (k + 1) * text_rows].astype(jnp.bfloat16), "dp", -k)
        for k in range(1, STEPS)
    ]
    d_weight, sent = sum_over_dp(local_weight, sent)

    grad_txt = txt_terms[:text_rows]
    for term in sent:
        grad_txt = grad_txt + term.astype(jnp.float32)
    inner_txt = jnp.sum(unit_txt * grad_txt, axis=1, keepdims=True)
    d_text = inv_txt * (grad_txt - unit_txt * inner_txt)
    return (d_weight, d_text)


def solution(mesh):
    in_specs = (P("dp", None), P(None, "emb"), P(("dp", "emb"), None), P(), P())
    out_specs = (P(None, "emb"), P(("dp", "emb"), None))
    return jax.shard_map(local, mesh=mesh, in_specs=in_specs, out_specs=out_specs, check_vma=False)
```

```python
import jax
import jax.numpy as jnp
from jax import lax
from jax.sharding import PartitionSpec as P

STEPS = 3
EPSILON = 1e-06
LANES = 128
ROWS = 8
PAIR = 2


def passed_along(array, axis, by):
    count = lax.axis_size(axis)
    return lax.ppermute(array, axis, [(i, (i + by) % count) for i in range(count)])


def to_partner(array):
    return lax.ppermute(array, "emb", [(i, i ^ 1) for i in range(lax.axis_size("emb"))])


def dp_groups(count):
    z_len = count // 4
    index = lambda hi, z, core: (hi * z_len + z) * 2 + core
    near = [
        [index(hi, z + dz, c) for hi in range(2) for dz in range(2) for c in range(2)]
        for z in range(0, z_len, 2)
    ]
    far = [list(members) for members in zip(*near)]
    return near, far


def swap(parts, axis, groups=None):
    return lax.all_to_all(parts, axis, 0, 0, axis_index_groups=groups)


def gathered(part, count, axis, groups=None):
    return swap(jnp.broadcast_to(part[None], (count,) + part.shape), axis, groups)


def summed(parts):
    return jnp.sum(parts.astype(jnp.float32), axis=0)


def sum_over_dp(grad_t, early):
    width, features = grad_t.shape
    tiles = features // LANES
    near, far = dp_groups(lax.axis_size("dp"))
    count = len(near[0])
    share = -(-tiles * width // (count * ROWS)) * ROWS
    rows = jnp.concatenate(
        [grad_t[:, LANES * t : LANES * (t + 1)] for t in range(tiles)], axis=0
    ).astype(jnp.bfloat16)
    rows = jnp.pad(rows, ((0, count * share - tiles * width), (0, 0)))
    part = summed(swap(rows.reshape(count, share, LANES), "dp", near)).astype(jnp.bfloat16)
    total = summed(lax.all_gather(part, "dp", axis=0, axis_index_groups=far)).astype(jnp.bfloat16)
    total, early = lax.optimization_barrier((total, early))
    whole = gathered(total, count, "dp", near).reshape(count * share, LANES)[: tiles * width]
    whole = whole.astype(jnp.float32).reshape(tiles, width, LANES)
    return jnp.swapaxes(whole, 1, 2).reshape(features, width), early


def unit_columns(values):
    wide = values.astype(jnp.float32)
    inverse = lax.rsqrt(jnp.sum(wide * wide, axis=0, keepdims=True) + EPSILON)
    return wide * inverse, inverse


def unit_rows(values):
    wide = values.astype(jnp.float32)
    inverse = lax.rsqrt(jnp.sum(wide * wide, axis=1, keepdims=True) + EPSILON)
    return wide * inverse, inverse


def local(img_feat, w_proj, txt_emb, logit_scale, logit_bias):
    image_rows, features = img_feat.shape
    text_rows = txt_emb.shape[0]
    width = w_proj.shape[1]
    members = lax.axis_size("emb")
    member = lax.axis_index("emb")
    half_rows = image_rows // PAIR
    first_row = (member % PAIR) * half_rows
    scale = logit_scale[0]
    offset = logit_bias[0]

    def slopes(texts, images, matches):
        cosines = jnp.dot(texts, images, preferred_element_type=jnp.float32)
        text = lax.broadcasted_iota(jnp.int32, cosines.shape, 0)
        image = lax.broadcasted_iota(jnp.int32, cosines.shape, 1)
        signs = jnp.where(matches(text, image), 1.0, -1.0)
        grads = -signs * jax.nn.sigmoid(-signs * (scale * cosines + offset))
        return cosines, grads.astype(jnp.bfloat16)

    partner_txt = to_partner(txt_emb)
    local_proj = lax.dot_general(
        w_proj, img_feat, (((0,), (1,)), ((), ())), preferred_element_type=jnp.float32
    ).astype(jnp.bfloat16)
    copies = jnp.broadcast_to(local_proj[None], (members,) + local_proj.shape)
    copies, txt_emb, partner_txt = lax.optimization_barrier((copies, txt_emb, partner_txt))
    unit_txt, inv_txt = unit_rows(txt_emb)
    pair_txt = jnp.concatenate([unit_txt, unit_rows(partner_txt)[0]], axis=0).astype(jnp.bfloat16)
    visitors = [pair_txt] + [passed_along(pair_txt, "dp", k) for k in range(1, STEPS)]
    projected = swap(copies, "emb").reshape(features, image_rows)

    mine = lax.dynamic_slice_in_dim(projected, first_row, half_rows, 1)
    unit_img, inv_img = unit_columns(mine)
    texts = lax.optimization_barrier(jnp.concatenate(visitors, axis=0))

    def pair_matches(text, image):
        row = image + first_row
        own = (text < text_rows) & (row == member * text_rows + text)
        other = (text >= text_rows) & (text < PAIR * text_rows)
        return own | (other & (row == (member ^ 1) * text_rows + text - text_rows))

    cosines, pair_grad = slopes(texts, unit_img.astype(jnp.bfloat16), pair_matches)
    inner_img = jnp.sum(pair_grad.astype(jnp.float32) * cosines, axis=0, keepdims=True)
    grad_img = lax.dot_general(
        texts, pair_grad, (((0,), (0,)), ((), ())), preferred_element_type=jnp.float32
    )
    grad_proj = (scale * inv_img) * (grad_img - unit_img * inner_img)
    parts = grad_proj.astype(jnp.bfloat16).reshape(members, width, half_rows)
    parts = swap(parts, "emb").reshape(members // PAIR, PAIR, width, half_rows)
    grad_part = summed(parts).astype(jnp.bfloat16)
    grad_part = jnp.concatenate([grad_part[h] for h in range(PAIR)], axis=1)
    local_weight = jnp.dot(grad_part, img_feat, preferred_element_type=jnp.float32)

    own_texts = jnp.concatenate([visitor[:text_rows] for visitor in visitors], axis=0)
    z_img = unit_columns(projected)[0].astype(jnp.bfloat16)
    own_grad = slopes(
        own_texts,
        z_img,
        lambda text, image: (text < text_rows) & (image == member * text_rows + text),
    )[1]
    txt_terms = scale * lax.dot_general(
        own_grad, z_img, (((1,), (1,)), ((), ())), preferred_element_type=jnp.float32
    )
    sent = [
        passed_along(txt_terms[k * text_rows : (k + 1) * text_rows].astype(jnp.bfloat16), "dp", -k)
        for k in range(1, STEPS)
    ]
    d_weight, sent = sum_over_dp(local_weight, sent)

    grad_txt = txt_terms[:text_rows]
    for term in sent:
        grad_txt = grad_txt + term.astype(jnp.float32)
    inner_txt = jnp.sum(unit_txt * grad_txt, axis=1, keepdims=True)
    d_text = inv_txt * (grad_txt - unit_txt * inner_txt)
    return (d_weight, d_text)


def solution(mesh):
    in_specs = (P("dp", None), P(None, "emb"), P(("dp", "emb"), None), P(), P())
    out_specs = (P(None, "emb"), P(("dp", "emb"), None))
    return jax.shard_map(local, mesh=mesh, in_specs=in_specs, out_specs=out_specs, check_vma=False)
```

```python
import jax
import jax.numpy as jnp
from jax import lax
from jax.sharding import PartitionSpec as P

STEPS = 3
EPSILON = 1e-06
LANES = 128
ROWS = 8
PAIR = 2


def passed_along(array, axis, by):
    count = lax.axis_size(axis)
    return lax.ppermute(array, axis, [(i, (i + by) % count) for i in range(count)])


def to_partner(array):
    return lax.ppermute(array, "emb", [(i, i ^ 1) for i in range(lax.axis_size("emb"))])


def dp_groups(count):
    z_len = count // 4
    index = lambda hi, z, core: (hi * z_len + z) * 2 + core
    near = [
        [index(hi, z + dz, c) for hi in range(2) for dz in range(2) for c in range(2)]
        for z in range(0, z_len, 2)
    ]
    far = [list(members) for members in zip(*near)]
    return near, far


def swap(parts, axis, groups=None):
    return lax.all_to_all(parts, axis, 0, 0, axis_index_groups=groups)


def gathered(part, count, axis, groups=None):
    return swap(jnp.broadcast_to(part[None], (count,) + part.shape), axis, groups)


def summed(parts):
    return jnp.sum(parts.astype(jnp.float32), axis=0)


def sum_over_dp(grad_t, early):
    width, features = grad_t.shape
    tiles = features // LANES
    near, far = dp_groups(lax.axis_size("dp"))
    count = len(near[0])
    share = -(-tiles * width // (count * ROWS)) * ROWS
    rows = jnp.concatenate(
        [grad_t[:, LANES * t : LANES * (t + 1)] for t in range(tiles)], axis=0
    ).astype(jnp.bfloat16)
    rows = jnp.pad(rows, ((0, count * share - tiles * width), (0, 0)))
    part = summed(swap(rows.reshape(count, share, LANES), "dp", near)).astype(jnp.bfloat16)
    part, early = lax.optimization_barrier((part, early))
    total = summed(lax.all_gather(part, "dp", axis=0, axis_index_groups=far)).astype(jnp.bfloat16)
    whole = gathered(total, count, "dp", near).reshape(count * share, LANES)[: tiles * width]
    whole = whole.astype(jnp.float32).reshape(tiles, width, LANES)
    return jnp.swapaxes(whole, 1, 2).reshape(features, width), early


def unit_columns(values):
    wide = values.astype(jnp.float32)
    inverse = lax.rsqrt(jnp.sum(wide * wide, axis=0, keepdims=True) + EPSILON)
    return wide * inverse, inverse


def unit_rows(values):
    wide = values.astype(jnp.float32)
    inverse = lax.rsqrt(jnp.sum(wide * wide, axis=1, keepdims=True) + EPSILON)
    return wide * inverse, inverse


def local(img_feat, w_proj, txt_emb, logit_scale, logit_bias):
    image_rows, features = img_feat.shape
    text_rows = txt_emb.shape[0]
    width = w_proj.shape[1]
    members = lax.axis_size("emb")
    member = lax.axis_index("emb")
    half_rows = image_rows // PAIR
    first_row = (member % PAIR) * half_rows
    scale = logit_scale[0]
    offset = logit_bias[0]

    def slopes(texts, images, matches):
        cosines = jnp.dot(texts, images, preferred_element_type=jnp.float32)
        text = lax.broadcasted_iota(jnp.int32, cosines.shape, 0)
        image = lax.broadcasted_iota(jnp.int32, cosines.shape, 1)
        signs = jnp.where(matches(text, image), 1.0, -1.0)
        grads = -signs * jax.nn.sigmoid(-signs * (scale * cosines + offset))
        return cosines, grads.astype(jnp.bfloat16)

    partner_txt = to_partner(txt_emb)
    local_proj = lax.dot_general(
        w_proj, img_feat, (((0,), (1,)), ((), ())), preferred_element_type=jnp.float32
    ).astype(jnp.bfloat16)
    copies = jnp.broadcast_to(local_proj[None], (members,) + local_proj.shape)
    copies, txt_emb, partner_txt = lax.optimization_barrier((copies, txt_emb, partner_txt))
    unit_txt, inv_txt = unit_rows(txt_emb)
    pair_txt = jnp.concatenate([unit_txt, unit_rows(partner_txt)[0]], axis=0).astype(jnp.bfloat16)
    visitors = [pair_txt] + [passed_along(pair_txt, "dp", k) for k in range(1, STEPS)]
    projected = swap(copies, "emb").reshape(features, image_rows)

    mine = lax.dynamic_slice_in_dim(projected, first_row, half_rows, 1)
    unit_img, inv_img = unit_columns(mine)
    texts = lax.optimization_barrier(jnp.concatenate(visitors, axis=0))

    def pair_matches(text, image):
        row = image + first_row
        own = (text < text_rows) & (row == member * text_rows + text)
        other = (text >= text_rows) & (text < PAIR * text_rows)
        return own | (other & (row == (member ^ 1) * text_rows + text - text_rows))

    cosines, pair_grad = slopes(texts, unit_img.astype(jnp.bfloat16), pair_matches)
    inner_img = jnp.sum(pair_grad.astype(jnp.float32) * cosines, axis=0, keepdims=True)
    grad_img = lax.dot_general(
        texts, pair_grad, (((0,), (0,)), ((), ())), preferred_element_type=jnp.float32
    )
    grad_proj = (scale * inv_img) * (grad_img - unit_img * inner_img)
    parts = grad_proj.astype(jnp.bfloat16).reshape(members, width, half_rows)
    parts = swap(parts, "emb").reshape(members // PAIR, PAIR, width, half_rows)
    grad_part = summed(parts).astype(jnp.bfloat16)
    grad_part = jnp.concatenate([grad_part[h] for h in range(PAIR)], axis=1)
    local_weight = jnp.dot(grad_part, img_feat, preferred_element_type=jnp.float32)

    own_texts = jnp.concatenate([visitor[:text_rows] for visitor in visitors], axis=0)
    z_img = unit_columns(projected)[0].astype(jnp.bfloat16)
    own_grad = slopes(
        own_texts,
        z_img,
        lambda text, image: (text < text_rows) & (image == member * text_rows + text),
    )[1]
    txt_terms = scale * lax.dot_general(
        own_grad, z_img, (((1,), (1,)), ((), ())), preferred_element_type=jnp.float32
    )
    d_weight, txt_terms = sum_over_dp(local_weight, txt_terms)
    sent = [
        passed_along(txt_terms[k * text_rows : (k + 1) * text_rows].astype(jnp.bfloat16), "dp", -k)
        for k in range(1, STEPS)
    ]

    grad_txt = txt_terms[:text_rows]
    for term in sent:
        grad_txt = grad_txt + term.astype(jnp.float32)
    inner_txt = jnp.sum(unit_txt * grad_txt, axis=1, keepdims=True)
    d_text = inv_txt * (grad_txt - unit_txt * inner_txt)
    return (d_weight, d_text)


def solution(mesh):
    in_specs = (P("dp", None), P(None, "emb"), P(("dp", "emb"), None), P(), P())
    out_specs = (P(None, "emb"), P(("dp", "emb"), None))
    return jax.shard_map(local, mesh=mesh, in_specs=in_specs, out_specs=out_specs, check_vma=False)
```

```python
import jax
import jax.numpy as jnp
from jax import lax
from jax.sharding import PartitionSpec as P

STEPS = 3
EPSILON = 1e-06
LANES = 128
ROWS = 8
PAIR = 2


def passed_along(array, axis, by):
    count = lax.axis_size(axis)
    return lax.ppermute(array, axis, [(i, (i + by) % count) for i in range(count)])


def to_partner(array):
    return lax.ppermute(array, "emb", [(i, i ^ 1) for i in range(lax.axis_size("emb"))])


def dp_groups(count):
    z_len = count // 4
    index = lambda hi, z, core: (hi * z_len + z) * 2 + core
    near = [
        [index(hi, z + dz, c) for hi in range(2) for dz in range(2) for c in range(2)]
        for z in range(0, z_len, 2)
    ]
    far = [list(members) for members in zip(*near)]
    return near, far


def swap(parts, axis, groups=None):
    return lax.all_to_all(parts, axis, 0, 0, axis_index_groups=groups)


def gathered(part, count, axis, groups=None):
    return swap(jnp.broadcast_to(part[None], (count,) + part.shape), axis, groups)


def summed(parts):
    return jnp.sum(parts.astype(jnp.float32), axis=0)


def sum_over_dp(grad_t, early):
    width, features = grad_t.shape
    tiles = features // LANES
    near, far = dp_groups(lax.axis_size("dp"))
    count = len(near[0])
    share = -(-tiles * width // (count * ROWS)) * ROWS
    rows = jnp.concatenate(
        [grad_t[:, LANES * t : LANES * (t + 1)] for t in range(tiles)], axis=0
    ).astype(jnp.bfloat16)
    rows = jnp.pad(rows, ((0, count * share - tiles * width), (0, 0)))
    part = summed(swap(rows.reshape(count, share, LANES), "dp", near)).astype(jnp.bfloat16)
    total = summed(lax.all_gather(part, "dp", axis=0, axis_index_groups=far)).astype(jnp.bfloat16)
    total, early = lax.optimization_barrier((total, early))
    whole = gathered(total, count, "dp", near).reshape(count * share, LANES)[: tiles * width]
    whole = whole.astype(jnp.float32).reshape(tiles, width, LANES)
    return jnp.swapaxes(whole, 1, 2).reshape(features, width), early


def unit_columns(values):
    wide = values.astype(jnp.float32)
    inverse = lax.rsqrt(jnp.sum(wide * wide, axis=0, keepdims=True) + EPSILON)
    return wide * inverse, inverse


def unit_rows(values):
    wide = values.astype(jnp.float32)
    inverse = lax.rsqrt(jnp.sum(wide * wide, axis=1, keepdims=True) + EPSILON)
    return wide * inverse, inverse


def local(img_feat, w_proj, txt_emb, logit_scale, logit_bias):
    image_rows, features = img_feat.shape
    text_rows = txt_emb.shape[0]
    width = w_proj.shape[1]
    members = lax.axis_size("emb")
    member = lax.axis_index("emb")
    half_rows = image_rows // PAIR
    first_row = (member % PAIR) * half_rows

    partner_txt = to_partner(txt_emb)
    local_proj = lax.dot_general(
        w_proj, img_feat, (((0,), (1,)), ((), ())), preferred_element_type=jnp.float32
    ).astype(jnp.bfloat16)
    copies = jnp.broadcast_to(local_proj[None], (members,) + local_proj.shape)
    copies, txt_emb, partner_txt, logit_scale, logit_bias = lax.optimization_barrier(
        (copies, txt_emb, partner_txt, logit_scale, logit_bias)
    )
    scale = logit_scale[0]
    offset = logit_bias[0]
    unit_txt, inv_txt = unit_rows(txt_emb)
    pair_txt = jnp.concatenate([unit_txt, unit_rows(partner_txt)[0]], axis=0).astype(jnp.bfloat16)
    visitors = [pair_txt] + [passed_along(pair_txt, "dp", k) for k in range(1, STEPS)]
    projected = swap(copies, "emb").reshape(features, image_rows)

    def slopes(texts, images, matches):
        cosines = jnp.dot(texts, images, preferred_element_type=jnp.float32)
        text = lax.broadcasted_iota(jnp.int32, cosines.shape, 0)
        image = lax.broadcasted_iota(jnp.int32, cosines.shape, 1)
        signs = jnp.where(matches(text, image), 1.0, -1.0)
        grads = -signs * jax.nn.sigmoid(-signs * (scale * cosines + offset))
        return cosines, grads.astype(jnp.bfloat16)

    mine = lax.dynamic_slice_in_dim(projected, first_row, half_rows, 1)
    unit_img, inv_img = unit_columns(mine)
    texts = lax.optimization_barrier(jnp.concatenate(visitors, axis=0))

    def pair_matches(text, image):
        row = image + first_row
        own = (text < text_rows) & (row == member * text_rows + text)
        other = (text >= text_rows) & (text < PAIR * text_rows)
        return own | (other & (row == (member ^ 1) * text_rows + text - text_rows))

    cosines, pair_grad = slopes(texts, unit_img.astype(jnp.bfloat16), pair_matches)
    inner_img = jnp.sum(pair_grad.astype(jnp.float32) * cosines, axis=0, keepdims=True)
    grad_img = lax.dot_general(
        texts, pair_grad, (((0,), (0,)), ((), ())), preferred_element_type=jnp.float32
    )
    grad_proj = (scale * inv_img) * (grad_img - unit_img * inner_img)
    parts = grad_proj.astype(jnp.bfloat16).reshape(members, width, half_rows)
    parts = swap(parts, "emb").reshape(members // PAIR, PAIR, width, half_rows)
    grad_part = summed(parts).astype(jnp.bfloat16)
    grad_part = jnp.concatenate([grad_part[h] for h in range(PAIR)], axis=1)
    local_weight = jnp.dot(grad_part, img_feat, preferred_element_type=jnp.float32)

    own_texts = jnp.concatenate([visitor[:text_rows] for visitor in visitors], axis=0)
    z_img = unit_columns(projected)[0].astype(jnp.bfloat16)
    own_grad = slopes(
        own_texts,
        z_img,
        lambda text, image: (text < text_rows) & (image == member * text_rows + text),
    )[1]
    txt_terms = scale * lax.dot_general(
        own_grad, z_img, (((1,), (1,)), ((), ())), preferred_element_type=jnp.float32
    )
    sent = [
        passed_along(txt_terms[k * text_rows : (k + 1) * text_rows].astype(jnp.bfloat16), "dp", -k)
        for k in range(1, STEPS)
    ]
    d_weight, sent = sum_over_dp(local_weight, sent)

    grad_txt = txt_terms[:text_rows]
    for term in sent:
        grad_txt = grad_txt + term.astype(jnp.float32)
    inner_txt = jnp.sum(unit_txt * grad_txt, axis=1, keepdims=True)
    d_text = inv_txt * (grad_txt - unit_txt * inner_txt)
    return (d_weight, d_text)


def solution(mesh):
    in_specs = (P("dp", None), P(None, "emb"), P(("dp", "emb"), None), P(), P())
    out_specs = (P(None, "emb"), P(("dp", "emb"), None))
    return jax.shard_map(local, mesh=mesh, in_specs=in_specs, out_specs=out_specs, check_vma=False)
```

```python
import jax
import jax.numpy as jnp
from jax import lax
from jax.sharding import PartitionSpec as P

STEPS = 3
EPSILON = 1e-06
LANES = 128
ROWS = 8
PAIR = 2


def passed_along(array, axis, by):
    count = lax.axis_size(axis)
    return lax.ppermute(array, axis, [(i, (i + by) % count) for i in range(count)])


def to_partner(array):
    return lax.ppermute(array, "emb", [(i, i ^ 1) for i in range(lax.axis_size("emb"))])


def dp_groups(count):
    z_len = count // 4
    index = lambda hi, z, core: (hi * z_len + z) * 2 + core
    near = [
        [index(hi, z + dz, c) for hi in range(2) for dz in range(2) for c in range(2)]
        for z in range(0, z_len, 2)
    ]
    far = [list(members) for members in zip(*near)]
    return near, far


def swap(parts, axis, groups=None):
    return lax.all_to_all(parts, axis, 0, 0, axis_index_groups=groups)


def gathered(part, count, axis, groups=None):
    return swap(jnp.broadcast_to(part[None], (count,) + part.shape), axis, groups)


def summed(parts):
    return jnp.sum(parts.astype(jnp.float32), axis=0)


def sum_over_dp(grad_t, early):
    width, features = grad_t.shape
    tiles = features // LANES
    near, far = dp_groups(lax.axis_size("dp"))
    count = len(near[0])
    share = -(-tiles * width // (count * ROWS)) * ROWS
    rows = jnp.concatenate(
        [grad_t[:, LANES * t : LANES * (t + 1)] for t in range(tiles)], axis=0
    ).astype(jnp.bfloat16)
    rows = jnp.pad(rows, ((0, count * share - tiles * width), (0, 0)))
    part = summed(swap(rows.reshape(count, share, LANES), "dp", near)).astype(jnp.bfloat16)
    total = summed(lax.all_gather(part, "dp", axis=0, axis_index_groups=far)).astype(jnp.bfloat16)
    total, early = lax.optimization_barrier((total, early))
    whole = gathered(total, count, "dp", near).reshape(count * share, LANES)[: tiles * width]
    whole = whole.astype(jnp.float32).reshape(tiles, width, LANES)
    return jnp.swapaxes(whole, 1, 2).reshape(features, width), early


def unit_columns(values):
    wide = values.astype(jnp.float32)
    inverse = lax.rsqrt(jnp.sum(wide * wide, axis=0, keepdims=True) + EPSILON)
    return wide * inverse, inverse


def unit_rows(values):
    wide = values.astype(jnp.float32)
    inverse = lax.rsqrt(jnp.sum(wide * wide, axis=1, keepdims=True) + EPSILON)
    return wide * inverse, inverse


def local(img_feat, w_proj, txt_emb, logit_scale, logit_bias):
    image_rows, features = img_feat.shape
    text_rows = txt_emb.shape[0]
    width = w_proj.shape[1]
    members = lax.axis_size("emb")
    member = lax.axis_index("emb")
    half_rows = image_rows // PAIR
    first_row = (member % PAIR) * half_rows

    partner_txt = to_partner(txt_emb)
    local_proj = lax.dot_general(
        w_proj, img_feat, (((0,), (1,)), ((), ())), preferred_element_type=jnp.float32
    ).astype(jnp.bfloat16)
    copies = jnp.broadcast_to(local_proj[None], (members,) + local_proj.shape)
    copies, txt_emb, logit_scale, logit_bias = lax.optimization_barrier(
        (copies, txt_emb, logit_scale, logit_bias)
    )
    scale = logit_scale[0]
    offset = logit_bias[0]
    unit_txt, inv_txt = unit_rows(txt_emb)
    pair_txt = jnp.concatenate([unit_txt, unit_rows(partner_txt)[0]], axis=0).astype(jnp.bfloat16)
    visitors = [pair_txt] + [passed_along(pair_txt, "dp", k) for k in range(1, STEPS)]
    projected = swap(copies, "emb").reshape(features, image_rows)

    def slopes(texts, images, matches):
        cosines = jnp.dot(texts, images, preferred_element_type=jnp.float32)
        text = lax.broadcasted_iota(jnp.int32, cosines.shape, 0)
        image = lax.broadcasted_iota(jnp.int32, cosines.shape, 1)
        signs = jnp.where(matches(text, image), 1.0, -1.0)
        grads = -signs * jax.nn.sigmoid(-signs * (scale * cosines + offset))
        return cosines, grads.astype(jnp.bfloat16)

    mine = lax.dynamic_slice_in_dim(projected, first_row, half_rows, 1)
    unit_img, inv_img = unit_columns(mine)
    texts = lax.optimization_barrier(jnp.concatenate(visitors, axis=0))

    def pair_matches(text, image):
        row = image + first_row
        own = (text < text_rows) & (row == member * text_rows + text)
        other = (text >= text_rows) & (text < PAIR * text_rows)
        return own | (other & (row == (member ^ 1) * text_rows + text - text_rows))

    cosines, pair_grad = slopes(texts, unit_img.astype(jnp.bfloat16), pair_matches)
    inner_img = jnp.sum(pair_grad.astype(jnp.float32) * cosines, axis=0, keepdims=True)
    grad_img = lax.dot_general(
        texts, pair_grad, (((0,), (0,)), ((), ())), preferred_element_type=jnp.float32
    )
    grad_proj = (scale * inv_img) * (grad_img - unit_img * inner_img)
    parts = grad_proj.astype(jnp.bfloat16).reshape(members, width, half_rows)
    parts = swap(parts, "emb").reshape(members // PAIR, PAIR, width, half_rows)
    grad_part = summed(parts).astype(jnp.bfloat16)
    grad_part = jnp.concatenate([grad_part[h] for h in range(PAIR)], axis=1)
    local_weight = jnp.dot(grad_part, img_feat, preferred_element_type=jnp.float32)

    own_texts = jnp.concatenate([visitor[:text_rows] for visitor in visitors], axis=0)
    z_img = unit_columns(projected)[0].astype(jnp.bfloat16)
    own_grad = slopes(
        own_texts,
        z_img,
        lambda text, image: (text < text_rows) & (image == member * text_rows + text),
    )[1]
    txt_terms = scale * lax.dot_general(
        own_grad, z_img, (((1,), (1,)), ((), ())), preferred_element_type=jnp.float32
    )
    sent = [
        passed_along(txt_terms[k * text_rows : (k + 1) * text_rows].astype(jnp.bfloat16), "dp", -k)
        for k in range(1, STEPS)
    ]
    d_weight, sent = sum_over_dp(local_weight, sent)

    grad_txt = txt_terms[:text_rows]
    for term in sent:
        grad_txt = grad_txt + term.astype(jnp.float32)
    inner_txt = jnp.sum(unit_txt * grad_txt, axis=1, keepdims=True)
    d_text = inv_txt * (grad_txt - unit_txt * inner_txt)
    return (d_weight, d_text)


def solution(mesh):
    in_specs = (P("dp", None), P(None, "emb"), P(("dp", "emb"), None), P(), P())
    out_specs = (P(None, "emb"), P(("dp", "emb"), None))
    return jax.shard_map(local, mesh=mesh, in_specs=in_specs, out_specs=out_specs, check_vma=False)
```

```python
import jax
import jax.numpy as jnp
from jax import lax
from jax.sharding import PartitionSpec as P

STEPS = 3
EPSILON = 1e-06
LANES = 128
ROWS = 8
PAIR = 2


def passed_along(array, axis, by):
    count = lax.axis_size(axis)
    return lax.ppermute(array, axis, [(i, (i + by) % count) for i in range(count)])


def to_partner(array):
    return lax.ppermute(array, "emb", [(i, i ^ 1) for i in range(lax.axis_size("emb"))])


def dp_groups(count):
    z_len = count // 4
    index = lambda hi, z, core: (hi * z_len + z) * 2 + core
    near = [
        [index(hi, z + dz, c) for hi in range(2) for dz in range(2) for c in range(2)]
        for z in range(0, z_len, 2)
    ]
    far = [list(members) for members in zip(*near)]
    return near, far


def swap(parts, axis, groups=None):
    return lax.all_to_all(parts, axis, 0, 0, axis_index_groups=groups)


def gathered(part, count, axis, groups=None):
    return swap(jnp.broadcast_to(part[None], (count,) + part.shape), axis, groups)


def summed(parts):
    return jnp.sum(parts.astype(jnp.float32), axis=0)


def sum_over_dp(grad_t, early):
    width, features = grad_t.shape
    tiles = features // LANES
    near, far = dp_groups(lax.axis_size("dp"))
    count = len(near[0])
    share = -(-tiles * width // (count * ROWS)) * ROWS
    rows = jnp.concatenate(
        [grad_t[:, LANES * t : LANES * (t + 1)] for t in range(tiles)], axis=0
    ).astype(jnp.bfloat16)
    rows = jnp.pad(rows, ((0, count * share - tiles * width), (0, 0)))
    part = summed(swap(rows.reshape(count, share, LANES), "dp", near)).astype(jnp.bfloat16)
    total = summed(lax.all_gather(part, "dp", axis=0, axis_index_groups=far)).astype(jnp.bfloat16)
    total, early = lax.optimization_barrier((total, early))
    whole = gathered(total, count, "dp", near).reshape(count * share, LANES)[: tiles * width]
    whole = whole.astype(jnp.float32).reshape(tiles, width, LANES)
    return jnp.swapaxes(whole, 1, 2).reshape(features, width), early


def unit_columns(values):
    wide = values.astype(jnp.float32)
    inverse = lax.rsqrt(jnp.sum(wide * wide, axis=0, keepdims=True) + EPSILON)
    return wide * inverse, inverse


def unit_rows(values):
    wide = values.astype(jnp.float32)
    inverse = lax.rsqrt(jnp.sum(wide * wide, axis=1, keepdims=True) + EPSILON)
    return wide * inverse, inverse


def local(img_feat, w_proj, txt_emb, logit_scale, logit_bias):
    image_rows, features = img_feat.shape
    text_rows = txt_emb.shape[0]
    width = w_proj.shape[1]
    members = lax.axis_size("emb")
    member = lax.axis_index("emb")
    half_rows = image_rows // PAIR
    first_row = (member % PAIR) * half_rows

    partner_txt = to_partner(txt_emb)
    local_proj = lax.dot_general(
        w_proj, img_feat, (((0,), (1,)), ((), ())), preferred_element_type=jnp.float32
    ).astype(jnp.bfloat16)
    copies = jnp.broadcast_to(local_proj[None], (members,) + local_proj.shape)
    copies, txt_emb, logit_scale, logit_bias = lax.optimization_barrier(
        (copies, txt_emb, logit_scale, logit_bias)
    )
    scale = logit_scale[0]
    offset = logit_bias[0]
    unit_txt, inv_txt = lax.optimization_barrier(unit_rows(txt_emb))
    pair_txt = jnp.concatenate([txt_emb, partner_txt], axis=0)
    visitors = [pair_txt] + [passed_along(pair_txt, "dp", k) for k in range(1, STEPS)]
    projected = swap(copies, "emb").reshape(features, image_rows)

    def slopes(texts, images, matches):
        cosines = jnp.dot(texts, images, preferred_element_type=jnp.float32)
        text = lax.broadcasted_iota(jnp.int32, cosines.shape, 0)
        image = lax.broadcasted_iota(jnp.int32, cosines.shape, 1)
        signs = jnp.where(matches(text, image), 1.0, -1.0)
        grads = -signs * jax.nn.sigmoid(-signs * (scale * cosines + offset))
        return cosines, grads.astype(jnp.bfloat16)

    mine = lax.dynamic_slice_in_dim(projected, first_row, half_rows, 1)
    unit_img, inv_img = unit_columns(mine)
    texts = unit_rows(jnp.concatenate(visitors, axis=0))[0].astype(jnp.bfloat16)
    texts = lax.optimization_barrier(texts)

    def pair_matches(text, image):
        row = image + first_row
        own = (text < text_rows) & (row == member * text_rows + text)
        other = (text >= text_rows) & (text < PAIR * text_rows)
        return own | (other & (row == (member ^ 1) * text_rows + text - text_rows))

    cosines, pair_grad = slopes(texts, unit_img.astype(jnp.bfloat16), pair_matches)
    inner_img = jnp.sum(pair_grad.astype(jnp.float32) * cosines, axis=0, keepdims=True)
    grad_img = lax.dot_general(
        texts, pair_grad, (((0,), (0,)), ((), ())), preferred_element_type=jnp.float32
    )
    grad_proj = (scale * inv_img) * (grad_img - unit_img * inner_img)
    parts = grad_proj.astype(jnp.bfloat16).reshape(members, width, half_rows)
    parts = swap(parts, "emb").reshape(members // PAIR, PAIR, width, half_rows)
    grad_part = summed(parts).astype(jnp.bfloat16)
    grad_part = jnp.concatenate([grad_part[h] for h in range(PAIR)], axis=1)
    local_weight = jnp.dot(grad_part, img_feat, preferred_element_type=jnp.float32)

    firsts = [k * PAIR * text_rows for k in range(STEPS)]
    own_texts = jnp.concatenate([texts[i : i + text_rows] for i in firsts], axis=0)
    z_img = unit_columns(projected)[0].astype(jnp.bfloat16)
    own_grad = slopes(
        own_texts,
        z_img,
        lambda text, image: (text < text_rows) & (image == member * text_rows + text),
    )[1]
    txt_terms = scale * lax.dot_general(
        own_grad, z_img, (((1,), (1,)), ((), ())), preferred_element_type=jnp.float32
    )
    sent = [
        passed_along(txt_terms[k * text_rows : (k + 1) * text_rows].astype(jnp.bfloat16), "dp", -k)
        for k in range(1, STEPS)
    ]
    d_weight, sent = sum_over_dp(local_weight, sent)

    grad_txt = txt_terms[:text_rows]
    for term in sent:
        grad_txt = grad_txt + term.astype(jnp.float32)
    inner_txt = jnp.sum(unit_txt * grad_txt, axis=1, keepdims=True)
    d_text = inv_txt * (grad_txt - unit_txt * inner_txt)
    return (d_weight, d_text)


def solution(mesh):
    in_specs = (P("dp", None), P(None, "emb"), P(("dp", "emb"), None), P(), P())
    out_specs = (P(None, "emb"), P(("dp", "emb"), None))
    return jax.shard_map(local, mesh=mesh, in_specs=in_specs, out_specs=out_specs, check_vma=False)
```
